32 devices in a mesh: parts: 2 (over y), term: 16 (over z, x, core).
Axes of the slice: x: 2, y: 2, z: 4, core: 2. Of those that a mesh axis runs over, the one named last changes fastest.
Arguments:
- wavefunction: bfloat16 [4096, 1024], P(('parts', 'term')), parts along dimension 0, may hold values from -6 to 6
- left_ops: bfloat16 [320, 512, 512], P(('parts', 'term')), parts along dimension 0, may hold values from -0.0390625 to 0.0390625
- right_ops: bfloat16 [320, 512, 512], P(('parts', 'term')), parts along dimension 0, may hold values from -0.25 to 0.25
- src_sector: int32 [320], P(('parts', 'term')), parts along dimension 0, may hold values from 0 to 3
- dst_sector: int32 [320], P(('parts', 'term')), parts along dimension 0, may hold values from 0 to 3
- live_terms: int32 [32], P(('parts', 'term')), parts along dimension 0, may hold values from 1 to 10, 96 in all
Outputs:
- sigma_pair: float32 [4096, 1024], P(('parts', 'term')), parts along dimension 0
The draws below stay inside these ranges and needn't reach their ends.
There are 2 independent parts, one for each index of `parts`. The reference program is written for one: setup_inputs(seed, part) draws one part's arguments, and reference() takes and returns one part's arrays. A program takes and returns all parts, laid end to end along the dimension named above; each array names one. Nothing has to cross between parts.
Inputs may be any that keep to these rules, and one draw needn't show every extreme that they name: Slots 0 to live_terms[g] - 1 of group g are live; the counts of one part sum to 96 and one group has all 10 live.
All inputs are finite; a program needn't handle non-finite values.
Results may differ from the reference program's by a relative error of at most 0.0029.
Values may be sent and summed in bfloat16 or wider, within the bound.
No kernel may reach another device: no remote copies, remote signals or barrier semaphores. Data moves between devices by JAX's collectives and lax.ppermute only.
A program may use at most 128 MiB of HBM per device.

```python
import math
import jax
import jax.numpy as jnp
import numpy as np
from jax import lax

BW = 512
NSEC = 4
E_DEV = 10
ROWS = 2048
TERMS = 160
LIVE_TOTAL = 96
N_TERM = 16


def touch_ends(values, key, least, largest):
    longest = values.shape.index(max(values.shape))
    spots = []
    for shift in (0, 1):
        where = [jax.random.randint(jax.random.fold_in(key, axis), (), 0, length) for axis, length in enumerate(values.shape)]
        where[longest] = (where[longest] + shift) % values.shape[longest]
        spots.append(tuple(where))
    return values.at[spots[0]].set(least).at[spots[1]].set(largest)


def levels(stream_key, extent, pieces, smallest, top_value):
    def one(dim, parts):
        draws = jax.random.uniform(jax.random.fold_in(jax.random.fold_in(stream_key, 6), dim), (parts,), jnp.float32, smallest / len(pieces), top_value / len(pieces))
        return jnp.repeat(jnp.exp(draws), extent[dim] // parts).reshape((-1,) + (1,) * (len(extent) - dim - 1))

    level = one(*pieces[0])
    for cut in pieces[1:]:
        level = level * one(*cut)
    return level


def split_up(amount, total, bound, slope):
    loads = [(1 << 20) // math.isqrt(standing ** slope) + 1 for standing in range(2, amount + 1)]
    rest, counts = total - bound - (amount - 1), [1] * (amount - 1)
    while rest > 0:
        movable = [i for i in range(amount - 1) if counts[i] < bound]
        whole, left = sum([loads[i] for i in movable]), rest
        for i in movable:
            extra = min(bound - counts[i], max(1, left * loads[i] // whole), rest)
            counts[i] = counts[i] + extra
            rest = rest - extra
    return np.array([bound] + counts)


def uneven(rng, count, total, bound, skew):
    if count == 2:
        one = jax.random.randint(rng, (), max(1, total - bound), min(bound, total - 1) + 1)
        return jnp.stack([one, total - one])
    lengths = jnp.asarray(split_up(count, total, bound, skew), jnp.int32)
    twos = (count - 1) // 2
    donor, receiver = lengths[1:1 + 2 * twos:2], lengths[2:2 + 2 * twos:2]
    room = jnp.minimum(donor - 1, bound - receiver)
    moved = jax.random.randint(jax.random.fold_in(rng, 1), (twos,), 0, 1 << 20) % (room + 1)
    lengths = lengths.at[1:1 + 2 * twos:2].set(donor - moved).at[2:2 + 2 * twos:2].set(receiver + moved)
    return lengths[jax.random.permutation(jax.random.fold_in(rng, 2), count)]


def scatter_about(stream_key, shape, deviation, limit, pieces=(), kind=jnp.bfloat16):
    values = deviation * jax.random.normal(stream_key, shape, jnp.float32)
    if pieces:
        values = values * levels(stream_key, shape, pieces, -0.22, 0.18)
    return jnp.clip(values, -limit, limit).astype(kind)


def setup_inputs(seed: int = 0, part: int = 0) -> dict:
    keys = jax.random.split(jax.random.key(seed), 7)
    own_keys = jax.random.split(jax.random.fold_in(keys[6], part), 7)
    wavefunction = scatter_about(own_keys[0], (ROWS, 2 * BW), 1.0, 6.0, ((0, 16),))
    left_ops = scatter_about(own_keys[1], (TERMS, BW, BW), (BW * E_DEV * N_TERM // NSEC) ** -0.5, 0.0390625, ((0, 16),))
    right_ops = scatter_about(own_keys[2], (TERMS, BW, BW), BW ** -0.5, 0.25, ((0, 16),))
    src_sector = touch_ends(jax.random.randint(own_keys[3], (TERMS,), 0, NSEC), jax.random.fold_in(own_keys[3], 1), 0, NSEC - 1).astype(jnp.int32)
    dst_sector = touch_ends(jax.random.randint(own_keys[4], (TERMS,), 0, NSEC), jax.random.fold_in(own_keys[4], 1), 0, NSEC - 1).astype(jnp.int32)
    live_terms = uneven(own_keys[5], N_TERM, LIVE_TOTAL, E_DEV, 2).astype(jnp.int32)
    return dict(wavefunction=wavefunction, left_ops=left_ops, right_ops=right_ops, src_sector=src_sector, dst_sector=dst_sector, live_terms=live_terms)


def reference(wavefunction, left_ops, right_ops, src_sector, dst_sector, live_terms):
    total_slots = left_ops.shape[0]
    slot_ids = jnp.arange(total_slots, dtype=jnp.int32)
    owner_ids = slot_ids // E_DEV
    alive = (slot_ids % E_DEV) < live_terms[owner_ids]

    def add_term(partial_value, inputs):
        left, right, source_id, target_id, flag = inputs
        src_block = lax.dynamic_slice_in_dim(wavefunction, (source_id * BW).astype(jnp.int32), BW, 0)
        left_mixed = jnp.dot(left, src_block, preferred_element_type=jnp.float32).astype(jnp.bfloat16)
        stacked = left_mixed.reshape(BW * 2, BW)
        result = jnp.dot(stacked, right.T, preferred_element_type=jnp.float32).reshape(BW, 2 * BW)
        result = jnp.where(flag, result, jnp.zeros_like(result))
        row_start = (target_id * BW).astype(jnp.int32)
        current = lax.dynamic_slice_in_dim(partial_value, row_start, BW, 0)
        return lax.dynamic_update_slice_in_dim(partial_value, current + result, row_start, 0), None

    initial = jnp.zeros((NSEC * BW, 2 * BW), jnp.float32)
    sigma_pair, unused = lax.scan(add_term, initial, (left_ops, right_ops, src_sector, dst_sector, alive))
    return sigma_pair
```

```python
import functools

import jax
import jax.numpy as jnp
from jax import lax
from jax.experimental import pallas as pl
from jax.experimental.pallas import tpu as pltpu
from jax.sharding import PartitionSpec as P

F32, BF16 = jnp.float32, jnp.bfloat16
CORES = 2
VMEM = 48 * 1024 * 1024
ANY = pl.BlockSpec(memory_space=pl.ANY)
SMEM = pl.BlockSpec(memory_space=pltpu.SMEM)
WHOLE = pl.BlockSpec(memory_space=pltpu.VMEM)


def list_slots(own, sib, field, sector, slots, found):
    def look(t, count):
        found[count] = t
        hit = jnp.logical_and(t < own[2 * slots], own[field * slots + t] == sector)
        count = count + hit.astype(jnp.int32)
        found[count] = t + slots
        hit = jnp.logical_and(t < sib[2 * slots], sib[field * slots + t] == sector)
        return count + hit.astype(jnp.int32)

    return lax.fori_loop(0, slots, look, jnp.int32(0))


def start_fetch(term, slots, own_hbm, sib_hbm, target, sem):
    @pl.when(term < slots)
    def _():
        pltpu.make_async_copy(own_hbm.at[term], target, sem).start()

    @pl.when(term >= slots)
    def _():
        pltpu.make_async_copy(sib_hbm.at[term - slots], target, sem).start()


def left_kernel(phase, *refs):
    (own, sib, where, here, others, left, left_sib), refs = refs[:7], refs[7:]
    mixed, found, source, lbuf, obuf, psem, lsem, osem = refs[-8:]
    slots, depth = left.shape[0], lbuf.shape[0]
    half = here.shape[1]
    bands = others.shape[0] + 1
    sector, band, core = where[phase], where[where.shape[0] - 2], where[where.shape[0] - 1]
    count = list_slots(own, sib, 0, sector, slots, found)
    copies = []
    for j in range(bands):
        b = lax.rem(band + j, bands)
        for i in range(CORES):
            c = core if i == 0 else 1 - core
            row = pl.multiple_of((b * CORES + c) * half, half)
            part = here.at[i] if j == 0 else others.at[j - 1, i]
            copies.append(pltpu.make_async_copy(part, source.at[pl.ds(row, half)], psem.at[j * CORES + i]))
    for copy in copies:
        copy.start()
    for i in range(depth - 1):
        @pl.when(i < count)
        def _():
            start_fetch(found[i], slots, left, left_sib, lbuf.at[i], lsem.at[i])
    for copy in copies:
        copy.wait()

    def out_copy(i):
        return pltpu.make_async_copy(obuf.at[lax.rem(i, 2)], mixed.at[found[i]], osem.at[lax.rem(i, 2)])

    def step(i, carry):
        ahead = i + depth - 1
        @pl.when(ahead < count)
        def _():
            k = lax.rem(ahead, depth)
            start_fetch(found[ahead], slots, left, left_sib, lbuf.at[k], lsem.at[k])

        k = lax.rem(i, depth)
        pltpu.make_async_copy(left.at[0], lbuf.at[k], lsem.at[k]).wait()

        @pl.when(i >= 2)
        def _():
            out_copy(i - 2).wait()

        obuf[lax.rem(i, 2)] = jnp.dot(lbuf[k], source[...], preferred_element_type=F32).astype(BF16)
        out_copy(i).start()
        return carry

    lax.fori_loop(0, count, step, 0)
    for back in (2, 1):
        @pl.when(count >= back)
        def _():
            out_copy(count - back).wait()


def right_kernel(phase, *refs):
    own, sib, where, mixed, right, right_sib, keep, send, found, acc, mbuf, rbuf, msem, rsem = refs
    slots, depth = right.shape[0], rbuf.shape[0]
    half = keep.shape[1]
    bands = send.shape[0] + 1
    sector, band, core = where[phase], where[where.shape[0] - 2], where[where.shape[0] - 1]
    count = list_slots(own, sib, 1, sector, slots, found)

    def fetch(i, k):
        term = found[i]
        pltpu.make_async_copy(mixed.at[term], mbuf.at[k], msem.at[k]).start()
        start_fetch(term, slots, right, right_sib, rbuf.at[k], rsem.at[k])

    for i in range(depth - 1):
        @pl.when(i < count)
        def _():
            fetch(i, i)
    acc[...] = jnp.zeros_like(acc)

    def step(i, carry):
        ahead = i + depth - 1
        @pl.when(ahead < count)
        def _():
            fetch(ahead, lax.rem(ahead, depth))

        k = lax.rem(i, depth)
        pltpu.make_async_copy(mixed.at[0], mbuf.at[k], msem.at[k]).wait()
        pltpu.make_async_copy(right.at[0], rbuf.at[k], rsem.at[k]).wait()
        acc[...] += lax.dot_general(mbuf[k], rbuf[k], (((1,), (1,)), ((), ())), preferred_element_type=F32)
        return carry

    lax.fori_loop(0, count, step, 0)
    for j in range(bands):
        b = lax.rem(band + j, bands)
        for i in range(CORES):
            c = core if i == 0 else 1 - core
            rows = acc[pl.ds(pl.multiple_of((b * CORES + c) * half, half), half)]
            if j == 0:
                keep[i] = rows
            else:
                send[j - 1, i] = rows.astype(BF16)


def local(devices, wavefunction, left, right, src, dst, live):
    slots, width = left.shape[0], left.shape[1]
    half = wavefunction.shape[0]
    sectors = half * devices // width
    bands = devices // (sectors * CORES)
    me = lax.axis_index("term")
    core, band, plane = me % CORES, (me // CORES) % bands, me // (CORES * bands)

    def shift(value, planes=0, band_step=0, flip=False):
        pairs = []
        for i in range(devices):
            c, b, a = i % CORES, (i // CORES) % bands, i // (CORES * bands)
            c = 1 - c if flip else c
            b, a = (b + band_step) % bands, (a + planes) % sectors
            pairs.append((i, (a * bands + b) * CORES + c))
        return lax.ppermute(value, "term", pairs)

    def bands_of(block):
        return jnp.stack([shift(block, band_step=-j) for j in range(1, bands)])

    own_meta = jnp.concatenate([src, dst, live])
    sib_meta = shift(own_meta, flip=True)
    columns = wavefunction.reshape(half, CORES, width)
    mine = lax.dynamic_index_in_dim(columns, core, 1, keepdims=False)
    theirs = lax.dynamic_index_in_dim(columns, 1 - core, 1, keepdims=False)
    chip_block = jnp.stack([mine, shift(theirs, flip=True)])
    left_sib = shift(left, flip=True)
    right_sib = shift(right, flip=True)

    src_order = [0, 1, 3, 2][:sectors] if sectors == 4 else list(range(sectors))
    dst_order = [2, 1, 3, 0] if sectors == 4 else list(range(1, sectors)) + [0]
    blocks = [shift(chip_block, planes=d) if d else chip_block for d in src_order]
    where_src = jnp.stack([(plane - d) % sectors for d in src_order] + [band, core]).astype(jnp.int32)
    where_dst = jnp.stack([(plane + d) % sectors for d in dst_order] + [band, core]).astype(jnp.int32)

    params = pltpu.CompilerParams(vmem_limit_bytes=VMEM)
    term_flops = 2 * width**3
    depth = 4
    mixed = None
    for phase in range(sectors):
        operands = [own_meta, sib_meta, where_src, blocks[phase], bands_of(blocks[phase]), left, left_sib]
        if mixed is not None:
            operands.append(mixed)
        mixed = pl.pallas_call(
            functools.partial(left_kernel, phase),
            out_shape=jax.ShapeDtypeStruct((CORES * slots, width, width), BF16),
            in_specs=[SMEM] * 3 + [ANY] * (len(operands) - 3),
            out_specs=ANY,
            scratch_shapes=[
                pltpu.SMEM((CORES * slots + 1,), jnp.int32),
                pltpu.VMEM((width, width), BF16),
                pltpu.VMEM((depth, width, width), BF16),
                pltpu.VMEM((2, width, width), BF16),
                pltpu.SemaphoreType.DMA((bands * CORES,)),
                pltpu.SemaphoreType.DMA((depth,)),
                pltpu.SemaphoreType.DMA((2,)),
            ],
            input_output_aliases={} if mixed is None else {7: 0},
            compiler_params=params,
            cost_estimate=pl.CostEstimate(flops=3 * term_flops, bytes_accessed=7 * width * width * 2, transcendentals=0),
            name="left_mix",
        )(*operands)

    totals = []
    for phase in range(sectors):
        d = dst_order[phase]
        keep, send = pl.pallas_call(
            functools.partial(right_kernel, phase),
            out_shape=(
                jax.ShapeDtypeStruct((CORES, half, width), F32),
                jax.ShapeDtypeStruct((bands - 1, CORES, half, width), BF16),
            ),
            in_specs=[SMEM] * 3 + [ANY] * 3,
            out_specs=(WHOLE, WHOLE),
            scratch_shapes=[
                pltpu.SMEM((CORES * slots + 1,), jnp.int32),
                pltpu.VMEM((width, width), F32),
                pltpu.VMEM((depth, width, width), BF16),
                pltpu.VMEM((depth, width, width), BF16),
                pltpu.SemaphoreType.DMA((depth,)),
                pltpu.SemaphoreType.DMA((depth,)),
            ],
            compiler_params=params,
            cost_estimate=pl.CostEstimate(flops=3 * term_flops, bytes_accessed=9 * width * width * 2, transcendentals=0),
            name="right_mix",
        )(own_meta, sib_meta, where_dst, mixed, right, right_sib)
        for j in range(1, bands):
            keep = keep + shift(send[j - 1], band_step=j).astype(F32)
        if d:
            keep = keep.astype(BF16)
            totals.append((shift(keep[0], planes=d), shift(keep[1], planes=d, flip=True)))
        else:
            totals.append((keep[0], shift(keep[1].astype(BF16), flip=True)))
    same = sum(t[0].astype(F32) for t in totals)
    cross = sum(t[1].astype(F32) for t in totals)
    first = core == 0
    return jnp.concatenate([jnp.where(first, same, cross), jnp.where(first, cross, same)], axis=1)


def solution(mesh):
    spec = P(("parts", "term"))
    return jax.shard_map(
        functools.partial(local, mesh.shape["term"]),
        mesh=mesh,
        in_specs=(spec,) * 6,
        out_specs=spec,
        check_vma=False,
    )
```

```python
import functools

import jax
import jax.numpy as jnp
from jax import lax
from jax.experimental import pallas as pl
from jax.experimental.pallas import tpu as pltpu
from jax.sharding import PartitionSpec as P

F32, BF16 = jnp.float32, jnp.bfloat16
CORES = 2
VMEM = 16 * 1024 * 1024
ANY = pl.BlockSpec(memory_space=pl.ANY)
SMEM = pl.BlockSpec(memory_space=pltpu.SMEM)
WHOLE = pl.BlockSpec(memory_space=pltpu.VMEM)


def list_slots(own, sib, field, sector, slots, found):
    def look(t, count):
        found[count] = t
        hit = jnp.logical_and(t < own[2 * slots], own[field * slots + t] == sector)
        count = count + hit.astype(jnp.int32)
        found[count] = t + slots
        hit = jnp.logical_and(t < sib[2 * slots], sib[field * slots + t] == sector)
        return count + hit.astype(jnp.int32)

    return lax.fori_loop(0, slots, look, jnp.int32(0))


def start_fetch(term, slots, own_hbm, sib_hbm, target, sem):
    @pl.when(term < slots)
    def _():
        pltpu.make_async_copy(own_hbm.at[term], target, sem).start()

    @pl.when(term >= slots)
    def _():
        pltpu.make_async_copy(sib_hbm.at[term - slots], target, sem).start()


def left_kernel(phase, *refs):
    (own, sib, where, here, others, left, left_sib), refs = refs[:7], refs[7:]
    mixed, found, source, lbuf, obuf, lsem, osem = refs[-7:]
    slots, depth = left.shape[0], lbuf.shape[0]
    half = here.shape[1]
    bands = others.shape[0] + 1
    sector, band, core = where[phase], where[where.shape[0] - 2], where[where.shape[0] - 1]
    count = list_slots(own, sib, 0, sector, slots, found)
    for i in range(depth - 1):
        @pl.when(i < count)
        def _():
            start_fetch(found[i], slots, left, left_sib, lbuf.at[i], lsem.at[i])
    for j in range(bands):
        b = lax.rem(band + j, bands)
        for i in range(CORES):
            c = core if i == 0 else 1 - core
            row = pl.multiple_of((b * CORES + c) * half, half)
            source[pl.ds(row, half)] = here[i] if j == 0 else others[j - 1, i]

    def out_copy(i):
        return pltpu.make_async_copy(obuf.at[lax.rem(i, 2)], mixed.at[found[i]], osem.at[lax.rem(i, 2)])

    def step(i, carry):
        ahead = i + depth - 1
        @pl.when(ahead < count)
        def _():
            k = lax.rem(ahead, depth)
            start_fetch(found[ahead], slots, left, left_sib, lbuf.at[k], lsem.at[k])

        k = lax.rem(i, depth)
        pltpu.make_async_copy(left.at[0], lbuf.at[k], lsem.at[k]).wait()

        @pl.when(i >= 2)
        def _():
            out_copy(i - 2).wait()

        obuf[lax.rem(i, 2)] = jnp.dot(lbuf[k], source[...], preferred_element_type=F32).astype(BF16)
        out_copy(i).start()
        return carry

    lax.fori_loop(0, count, step, 0)
    for back in (2, 1):
        @pl.when(count >= back)
        def _():
            out_copy(count - back).wait()


def right_kernel(phase, *refs):
    own, sib, where, mixed, right, right_sib, keep, send, found, acc, mbuf, rbuf, msem, rsem = refs
    slots, depth = right.shape[0], rbuf.shape[0]
    half = keep.shape[1]
    bands = send.shape[0] + 1
    sector, band, core = where[phase], where[where.shape[0] - 2], where[where.shape[0] - 1]
    count = list_slots(own, sib, 1, sector, slots, found)

    def fetch(i, k):
        term = found[i]
        pltpu.make_async_copy(mixed.at[term], mbuf.at[k], msem.at[k]).start()
        start_fetch(term, slots, right, right_sib, rbuf.at[k], rsem.at[k])

    for i in range(depth - 1):
        @pl.when(i < count)
        def _():
            fetch(i, i)
    acc[...] = jnp.zeros_like(acc)

    def step(i, carry):
        ahead = i + depth - 1
        @pl.when(ahead < count)
        def _():
            fetch(ahead, lax.rem(ahead, depth))

        k = lax.rem(i, depth)
        pltpu.make_async_copy(mixed.at[0], mbuf.at[k], msem.at[k]).wait()
        pltpu.make_async_copy(right.at[0], rbuf.at[k], rsem.at[k]).wait()
        acc[...] += lax.dot_general(mbuf[k], rbuf[k], (((1,), (1,)), ((), ())), preferred_element_type=F32)
        return carry

    lax.fori_loop(0, count, step, 0)
    for j in range(bands):
        b = lax.rem(band + j, bands)
        for i in range(CORES):
            c = core if i == 0 else 1 - core
            rows = acc[pl.ds(pl.multiple_of((b * CORES + c) * half, half), half)]
            if j == 0:
                keep[i] = rows
            else:
                send[j - 1, i] = rows.astype(BF16)


def local(devices, wavefunction, left, right, src, dst, live):
    slots, width = left.shape[0], left.shape[1]
    half = wavefunction.shape[0]
    sectors = half * devices // width
    bands = devices // (sectors * CORES)
    assert sectors == 4
    me = lax.axis_index("term")
    core, band, plane = me % CORES, (me // CORES) % bands, me // (CORES * bands)

    def move(value, to_plane=lambda a: a, band_step=0, flip=False):
        pairs = []
        for i in range(devices):
            c, b, a = i % CORES, (i // CORES) % bands, i // (CORES * bands)
            c = 1 - c if flip else c
            pairs.append((i, (to_plane(a) * bands + (b + band_step) % bands) * CORES + c))
        return lax.ppermute(value, "term", pairs)

    def beside(a):
        return a ^ 1

    def mirror(a):
        return 3 - a

    def bands_of(block):
        return jnp.stack([move(block, band_step=-j) for j in range(1, bands)])

    own_meta = jnp.concatenate([src, dst, live])
    sib_meta = move(own_meta, flip=True)
    mine = lax.dynamic_slice_in_dim(wavefunction, core * width, width, 1)
    theirs = lax.dynamic_slice_in_dim(wavefunction, (1 - core) * width, width, 1)
    from_sib = move(theirs, flip=True)
    left_sib, from_sib = lax.optimization_barrier((left, from_sib))
    left_sib = move(left_sib, flip=True)
    own_block = jnp.stack([mine, from_sib])
    mirror_block = move(own_block, mirror)
    beside_block = move(own_block, beside)
    right_sib, mirror_block = lax.optimization_barrier((right, mirror_block))
    right_sib = move(right_sib, flip=True)
    blocks = [own_block, beside_block, mirror_block, None]
    partner = plane ^ 1
    where_src = jnp.stack([plane, partner, 3 - plane, 3 - partner, band, core]).astype(jnp.int32)
    where_dst = jnp.stack([3 - partner, 3 - plane, partner, plane, band, core]).astype(jnp.int32)

    params = pltpu.CompilerParams(vmem_limit_bytes=VMEM)
    cost = pl.CostEstimate(flops=4 * 10**9, bytes_accessed=7 * width * width * 2, transcendentals=0)
    depth = 4
    mixed = None
    for phase in range(sectors):
        if phase == 1:
            forward, mixed = lax.optimization_barrier((mirror_block, mixed))
            blocks[3] = move(forward, beside)
        if phase == 2:
            blocks[3], mixed = lax.optimization_barrier((blocks[3], mixed))
        operands = [own_meta, sib_meta, where_src, blocks[phase], bands_of(blocks[phase]), left, left_sib]
        if mixed is not None:
            operands.append(mixed)
        mixed = pl.pallas_call(
            functools.partial(left_kernel, phase),
            out_shape=jax.ShapeDtypeStruct((CORES * slots, width, width), BF16),
            in_specs=[SMEM] * 3 + [WHOLE] * 2 + [ANY] * (len(operands) - 5),
            out_specs=ANY,
            scratch_shapes=[
                pltpu.SMEM((CORES * slots + 1,), jnp.int32),
                pltpu.VMEM((width, width), BF16),
                pltpu.VMEM((depth, width, width), BF16),
                pltpu.VMEM((2, width, width), BF16),
                pltpu.SemaphoreType.DMA((depth,)),
                pltpu.SemaphoreType.DMA((2,)),
            ],
            input_output_aliases={} if mixed is None else {7: 0},
            compiler_params=params,
            cost_estimate=cost,
            name="left_mix",
        )(*operands)

    def right_mix(phase, meta):
        keep, send = pl.pallas_call(
            functools.partial(right_kernel, phase),
            out_shape=(
                jax.ShapeDtypeStruct((CORES, half, width), F32),
                jax.ShapeDtypeStruct((bands - 1, CORES, half, width), BF16),
            ),
            in_specs=[SMEM] * 3 + [ANY] * 3,
            out_specs=(WHOLE, WHOLE),
            scratch_shapes=[
                pltpu.SMEM((CORES * slots + 1,), jnp.int32),
                pltpu.VMEM((width, width), F32),
                pltpu.VMEM((depth, width, width), BF16),
                pltpu.VMEM((depth, width, width), BF16),
                pltpu.SemaphoreType.DMA((depth,)),
                pltpu.SemaphoreType.DMA((depth,)),
            ],
            compiler_params=params,
            cost_estimate=cost,
            name="right_mix",
        )(meta, sib_meta, where_dst, mixed, right, right_sib)
        for j in range(1, bands):
            keep = keep + move(send[j - 1], band_step=j).astype(F32)
        return keep

    beside_far = right_mix(0, own_meta).astype(BF16)
    mirrored = right_mix(1, own_meta)
    meta, beside_far = lax.optimization_barrier((own_meta, beside_far))
    mirrored = (mirrored + move(beside_far, beside).astype(F32)).astype(BF16)
    beside_near = right_mix(2, meta).astype(BF16)
    total = right_mix(3, meta) + move(mirrored, mirror).astype(F32) + move(beside_near, beside).astype(F32)
    same, cross = total[0], move(total[1], flip=True)
    first = core == 0
    return jnp.concatenate([jnp.where(first, same, cross), jnp.where(first, cross, same)], axis=1)


def solution(mesh):
    spec = P(("parts", "term"))
    return jax.shard_map(
        functools.partial(local, mesh.shape["term"]),
        mesh=mesh,
        in_specs=(spec,) * 6,
        out_specs=spec,
        check_vma=False,
    )
```

```python
import functools

import jax
import jax.numpy as jnp
from jax import lax
from jax.experimental import pallas as pl
from jax.experimental.pallas import tpu as pltpu
from jax.sharding import PartitionSpec as P

F32, BF16 = jnp.float32, jnp.bfloat16
CORES = 2
HALVES = 2
VMEM = 16 * 1024 * 1024
ANY = pl.BlockSpec(memory_space=pl.ANY)
SMEM = pl.BlockSpec(memory_space=pltpu.SMEM)
WHOLE = pl.BlockSpec(memory_space=pltpu.VMEM)


def list_slots(own, sib, field, sector, slots, found):
    def look(t, count):
        found[count] = t
        hit = jnp.logical_and(t < own[2 * slots], own[field * slots + t] == sector)
        count = count + hit.astype(jnp.int32)
        found[count] = t + slots
        hit = jnp.logical_and(t < sib[2 * slots], sib[field * slots + t] == sector)
        return count + hit.astype(jnp.int32)

    return lax.fori_loop(0, slots, look, jnp.int32(0))


def start_fetch(term, slots, own_hbm, sib_hbm, target, sem):
    @pl.when(term < slots)
    def _():
        pltpu.make_async_copy(own_hbm.at[term], target, sem).start()

    @pl.when(term >= slots)
    def _():
        pltpu.make_async_copy(sib_hbm.at[term - slots], target, sem).start()


def left_kernel(own, sib, source, left, left_sib, mixed, lbuf, obuf, lsem, osem):
    slots, depth, width = left.shape[0], lbuf.shape[0], left.shape[1]
    mine = own[2 * slots]
    count = mine + sib[2 * slots]

    def term(i):
        return jnp.where(i < mine, i, i - mine + slots)

    for i in range(depth - 1):
        @pl.when(i < count)
        def _():
            start_fetch(term(i), slots, left, left_sib, lbuf.at[i], lsem.at[i])

    def out_copy(i):
        return pltpu.make_async_copy(obuf.at[lax.rem(i, 2)], mixed.at[term(i)], osem.at[lax.rem(i, 2)])

    def step(i, carry):
        ahead = i + depth - 1
        @pl.when(ahead < count)
        def _():
            k = lax.rem(ahead, depth)
            start_fetch(term(ahead), slots, left, left_sib, lbuf.at[k], lsem.at[k])

        k = lax.rem(i, depth)
        pltpu.make_async_copy(left.at[0], lbuf.at[k], lsem.at[k]).wait()

        @pl.when(i >= 2)
        def _():
            out_copy(i - 2).wait()

        sector = jnp.where(i < mine, own[jnp.minimum(i, slots - 1)], sib[jnp.clip(i - mine, 0, slots - 1)])
        block = source[pl.ds(pl.multiple_of(sector * width, width), width)]
        obuf[lax.rem(i, 2)] = jnp.dot(lbuf[k], block, preferred_element_type=F32).astype(BF16)
        out_copy(i).start()
        return carry

    lax.fori_loop(0, count, step, 0)
    for back in (2, 1):
        @pl.when(count >= back)
        def _():
            out_copy(count - back).wait()


def right_kernel(phase, *refs):
    own, sib, where, mixed_a, mixed_b, right, right_sib, keep, send, found, acc, mbuf, rbuf, msem, rsem = refs
    slots, depth = right.shape[0], rbuf.shape[0]
    half = keep.shape[1]
    bands = send.shape[0] + 1
    sector, band, core = where[phase], where[where.shape[0] - 2], where[where.shape[0] - 1]
    count = list_slots(own, sib, 1, sector, slots, found)

    def fetch(i, k):
        term = found[i]
        for h, mixed in enumerate((mixed_a, mixed_b)):
            pltpu.make_async_copy(mixed.at[term], mbuf.at[k, h], msem.at[k, h]).start()
        start_fetch(term, slots, right, right_sib, rbuf.at[k], rsem.at[k])

    for i in range(depth - 1):
        @pl.when(i < count)
        def _():
            fetch(i, i)
    acc[...] = jnp.zeros_like(acc)

    def step(i, carry):
        ahead = i + depth - 1
        @pl.when(ahead < count)
        def _():
            fetch(ahead, lax.rem(ahead, depth))

        k = lax.rem(i, depth)
        for h, mixed in enumerate((mixed_a, mixed_b)):
            pltpu.make_async_copy(mixed.at[0], mbuf.at[k, h], msem.at[k, h]).wait()
        pltpu.make_async_copy(right.at[0], rbuf.at[k], rsem.at[k]).wait()
        part = mbuf.shape[3]
        acc[...] += sum(
            lax.dot_general(
                mbuf[k, h], rbuf[k, :, h * part : (h + 1) * part], (((1,), (1,)), ((), ())), preferred_element_type=F32
            )
            for h in range(HALVES)
        )
        return carry

    lax.fori_loop(0, count, step, 0)
    for j in range(bands):
        b = lax.rem(band + j, bands)
        for i in range(CORES):
            c = core if i == 0 else 1 - core
            rows = acc[pl.ds(pl.multiple_of((b * CORES + c) * half, half), half)]
            if j == 0:
                keep[i] = rows
            else:
                send[j - 1, i] = rows.astype(BF16)


def local(devices, wavefunction, left, right, src, dst, live):
    slots, width = left.shape[0], left.shape[1]
    half = wavefunction.shape[0]
    sectors = half * devices // width
    bands = devices // (sectors * CORES)
    assert sectors == 4
    me = lax.axis_index("term")
    core, band, plane = me % CORES, (me // CORES) % bands, me // (CORES * bands)

    def move(value, to_plane=lambda a: a, band_step=0, flip=False):
        pairs = []
        for i in range(devices):
            c, b, a = i % CORES, (i // CORES) % bands, i // (CORES * bands)
            c = 1 - c if flip else c
            pairs.append((i, (to_plane(a) * bands + (b + band_step) % bands) * CORES + c))
        return lax.ppermute(value, "term", pairs)

    def beside(a):
        return a ^ 1

    def mirror(a):
        return 3 - a

    own_meta = jnp.concatenate([src, dst, live])
    sib_meta = move(own_meta, flip=True)
    mine = lax.dynamic_slice_in_dim(wavefunction, core * width, width, 1)
    theirs = lax.dynamic_slice_in_dim(wavefunction, (1 - core) * width, width, 1)
    from_sib = move(theirs, flip=True)
    left_sib, right_sib, from_sib = lax.optimization_barrier((left, right, from_sib))
    left_sib, right_sib = move(left_sib, flip=True), move(right_sib, flip=True)
    pair = jnp.stack([jnp.where(core == 0, mine, from_sib), jnp.where(core == 0, from_sib, mine)])
    part = width // HALVES
    groups = [[c + CORES * chip for chip in range(devices // CORES)] for c in range(CORES)]
    sources = [
        lax.all_gather(
            pair[:, :, h * part : (h + 1) * part].reshape(CORES * half, part),
            "term", axis=0, tiled=True, axis_index_groups=groups,
        )
        for h in range(HALVES)
    ]
    partner = plane ^ 1
    where_dst = jnp.stack([3 - partner, 3 - plane, partner, plane, band, core]).astype(jnp.int32)

    params = pltpu.CompilerParams(vmem_limit_bytes=VMEM)
    cost = pl.CostEstimate(flops=4 * 10**9, bytes_accessed=7 * width * width * 2, transcendentals=0)
    depth = 4
    mixed = [
        pl.pallas_call(
            left_kernel,
            out_shape=jax.ShapeDtypeStruct((CORES * slots, width, part), BF16),
            in_specs=[SMEM] * 2 + [WHOLE] + [ANY] * 2,
            out_specs=ANY,
            scratch_shapes=[
                pltpu.VMEM((depth, width, width), BF16),
                pltpu.VMEM((2, width, part), BF16),
                pltpu.SemaphoreType.DMA((depth,)),
                pltpu.SemaphoreType.DMA((2,)),
            ],
            compiler_params=params,
            cost_estimate=cost,
            name="left_mix",
        )(own_meta, sib_meta, source, left, left_sib)
        for source in sources
    ]

    def right_mix(phase, meta):
        keep, send = pl.pallas_call(
            functools.partial(right_kernel, phase),
            out_shape=(
                jax.ShapeDtypeStruct((CORES, half, width), F32),
                jax.ShapeDtypeStruct((bands - 1, CORES, half, width), BF16),
            ),
            in_specs=[SMEM] * 3 + [ANY] * 4,
            out_specs=(WHOLE, WHOLE),
            scratch_shapes=[
                pltpu.SMEM((CORES * slots + 1,), jnp.int32),
                pltpu.VMEM((width, width), F32),
                pltpu.VMEM((depth, HALVES, width, part), BF16),
                pltpu.VMEM((depth, width, width), BF16),
                pltpu.SemaphoreType.DMA((depth, HALVES)),
                pltpu.SemaphoreType.DMA((depth,)),
            ],
            compiler_params=params,
            cost_estimate=cost,
            name="right_mix",
        )(meta, sib_meta, where_dst, *mixed, right, right_sib)
        for j in range(1, bands):
            keep = keep + move(send[j - 1], band_step=j).astype(F32)
        return keep

    beside_far = right_mix(0, own_meta).astype(BF16)
    mirrored = right_mix(1, own_meta)
    meta, beside_far = lax.optimization_barrier((own_meta, beside_far))
    mirrored = (mirrored + move(beside_far, beside).astype(F32)).astype(BF16)
    beside_near = right_mix(2, meta).astype(BF16)
    total = right_mix(3, meta) + move(mirrored, mirror).astype(F32) + move(beside_near, beside).astype(F32)
    same, cross = total[0], move(total[1], flip=True)
    first = core == 0
    return jnp.concatenate([jnp.where(first, same, cross), jnp.where(first, cross, same)], axis=1)


def solution(mesh):
    spec = P(("parts", "term"))
    return jax.shard_map(
        functools.partial(local, mesh.shape["term"]),
        mesh=mesh,
        in_specs=(spec,) * 6,
        out_specs=spec,
        check_vma=False,
    )
```

```python
import functools

import jax
import jax.numpy as jnp
from jax import lax
from jax.experimental import pallas as pl
from jax.experimental.pallas import tpu as pltpu
from jax.sharding import PartitionSpec as P

F32, BF16 = jnp.float32, jnp.bfloat16
CORES = 2
VMEM = 24 * 1024 * 1024
ANY = pl.BlockSpec(memory_space=pl.ANY)
SMEM = pl.BlockSpec(memory_space=pltpu.SMEM)
WHOLE = pl.BlockSpec(memory_space=pltpu.VMEM)


def list_slots(own, sib, field, sector, slots, found):
    count = jnp.int32(0)
    for core, meta in enumerate((own, sib)):
        live = meta[2 * slots]
        for t in range(slots):
            found[count] = core * slots + t
            hit = jnp.logical_and(t < live, meta[field * slots + t] == sector)
            count = count + hit.astype(jnp.int32)
    return count


def in_pairs(count, depth, fetch, wait, work):
    for i in range(depth - 2):
        @pl.when(i < count)
        def _():
            fetch(i, i)

    def pair(p, carry):
        i = 2 * p
        for ahead in (i + depth - 2, i + depth - 1):
            @pl.when(ahead < count)
            def _():
                fetch(ahead, lax.rem(ahead, depth))
        spots = [lax.rem(i, depth), lax.rem(i, depth) + 1]
        for k in spots:
            wait(k)
        work((i, i + 1), spots)
        return carry

    lax.fori_loop(0, count // 2, pair, 0)

    @pl.when(count % 2 == 1)
    def _():
        k = lax.rem(count - 1, depth)
        wait(k)
        work((count - 1,), (k,))


def start_fetch(term, slots, own_hbm, sib_hbm, target, sem):
    @pl.when(term < slots)
    def _():
        pltpu.make_async_copy(own_hbm.at[term], target, sem).start()

    @pl.when(term >= slots)
    def _():
        pltpu.make_async_copy(sib_hbm.at[term - slots], target, sem).start()


def left_kernel(phase, *refs):
    (own, sib, where, here, others, left, left_sib), refs = refs[:7], refs[7:]
    mixed, found, source, lbuf, obuf, lsem, osem = refs[-7:]
    slots, depth, outs = left.shape[0], lbuf.shape[0], obuf.shape[0]
    half = here.shape[1]
    bands = others.shape[0] + 1
    sector, band, core = where[phase], where[where.shape[0] - 2], where[where.shape[0] - 1]
    count = list_slots(own, sib, 0, sector, slots, found)

    def fetch(i, k):
        start_fetch(found[i], slots, left, left_sib, lbuf.at[k], lsem.at[k])

    def wait(k):
        pltpu.make_async_copy(left.at[0], lbuf.at[k], lsem.at[k]).wait()

    def out_copy(i, o):
        return pltpu.make_async_copy(obuf.at[o], mixed.at[found[i]], osem.at[o])

    def work(items, spots):
        for i, k in zip(items, spots):
            o = lax.rem(i, outs)

            @pl.when(i >= outs)
            def _():
                out_copy(i - outs, o).wait()

            obuf[o] = jnp.dot(lbuf[k], source[...], preferred_element_type=F32).astype(BF16)
            out_copy(i, o).start()

    for j in range(bands):
        b = lax.rem(band + j, bands)
        for i in range(CORES):
            c = core if i == 0 else 1 - core
            row = pl.multiple_of((b * CORES + c) * half, half)
            source[pl.ds(row, half)] = here[i] if j == 0 else others[j - 1, i]
    in_pairs(count, depth, fetch, wait, work)
    for back in range(outs, 0, -1):
        @pl.when(count >= back)
        def _():
            out_copy(count - back, lax.rem(count - back, outs)).wait()


def right_kernel(phase, own, sib, where, mixed, right, right_sib, keep, send, found, acc, rbuf, rsem):
    slots, depth = right.shape[0], rbuf.shape[0]
    half = keep.shape[1]
    bands = send.shape[0] + 1
    sector, band, core = where[phase], where[where.shape[0] - 2], where[where.shape[0] - 1]
    count = list_slots(own, sib, 1, sector, slots, found)

    def fetch(i, k):
        start_fetch(found[i], slots, right, right_sib, rbuf.at[k], rsem.at[k])

    def wait(k):
        pltpu.make_async_copy(right.at[0], rbuf.at[k], rsem.at[k]).wait()

    def work(items, spots):
        acc[...] += sum(
            lax.dot_general(mixed[found[i]], rbuf[k], (((1,), (1,)), ((), ())), preferred_element_type=F32)
            for i, k in zip(items, spots)
        )

    acc[...] = jnp.zeros_like(acc)
    in_pairs(count, depth, fetch, wait, work)
    for j in range(bands):
        b = lax.rem(band + j, bands)
        for i in range(CORES):
            c = core if i == 0 else 1 - core
            rows = acc[pl.ds(pl.multiple_of((b * CORES + c) * half, half), half)]
            if j == 0:
                keep[i] = rows
            else:
                send[j - 1, i] = rows.astype(BF16)


def local(devices, wavefunction, left, right, src, dst, live):
    slots, width = left.shape[0], left.shape[1]
    half = wavefunction.shape[0]
    sectors = half * devices // width
    bands = devices // (sectors * CORES)
    assert sectors == 4
    me = lax.axis_index("term")
    core, band, plane = me % CORES, (me // CORES) % bands, me // (CORES * bands)

    def move(value, to_plane=lambda a: a, band_step=0, flip=False):
        pairs = []
        for i in range(devices):
            c, b, a = i % CORES, (i // CORES) % bands, i // (CORES * bands)
            c = 1 - c if flip else c
            pairs.append((i, (to_plane(a) * bands + (b + band_step) % bands) * CORES + c))
        return lax.ppermute(value, "term", pairs)

    def beside(a):
        return a ^ 1

    def mirror(a):
        return 3 - a

    def bands_of(block):
        return jnp.stack([move(block, band_step=-j) for j in range(1, bands)])

    own_meta = jnp.concatenate([src, dst, live])
    sib_meta = move(own_meta, flip=True)
    mine = lax.dynamic_slice_in_dim(wavefunction, core * width, width, 1)
    theirs = lax.dynamic_slice_in_dim(wavefunction, (1 - core) * width, width, 1)
    from_sib = move(theirs, flip=True)
    left_sib, from_sib = lax.optimization_barrier((left, from_sib))
    left_sib = move(left_sib, flip=True)
    own_block = jnp.stack([mine, from_sib])
    mirror_block = move(own_block, mirror)
    beside_block, own_bands = lax.optimization_barrier((move(own_block, beside), bands_of(own_block)))
    beside_bands = bands_of(beside_block)
    mirror_block, right_sib, beside_block, own_bands = lax.optimization_barrier(
        (mirror_block, right, beside_block, own_bands)
    )
    right_sib = move(right_sib, flip=True)
    mirror_bands = bands_of(mirror_block)
    far_block = move(mirror_block, beside)
    blocks = [
        (own_block, own_bands),
        (beside_block, beside_bands),
        (mirror_block, mirror_bands),
        (far_block, bands_of(far_block)),
    ]
    partner = plane ^ 1
    where_src = jnp.stack([plane, partner, 3 - plane, 3 - partner, band, core]).astype(jnp.int32)
    where_dst = jnp.stack([3 - partner, 3 - plane, partner, plane, band, core]).astype(jnp.int32)

    params = pltpu.CompilerParams(vmem_limit_bytes=VMEM)
    cost = pl.CostEstimate(flops=3 * 10**9, bytes_accessed=7 * width * width * 2, transcendentals=0)
    depth = 8
    mixed = None
    for phase in range(sectors):
        operands = [own_meta, sib_meta, where_src, *blocks[phase], left, left_sib]
        if mixed is not None:
            operands.append(mixed)
        mixed = pl.pallas_call(
            functools.partial(left_kernel, phase),
            out_shape=jax.ShapeDtypeStruct((CORES * slots, width, width), BF16),
            in_specs=[SMEM] * 3 + [WHOLE] * 2 + [ANY] * (len(operands) - 5),
            out_specs=ANY,
            scratch_shapes=[
                pltpu.SMEM((CORES * slots + 1,), jnp.int32),
                pltpu.VMEM((width, width), BF16),
                pltpu.VMEM((depth, width, width), BF16),
                pltpu.VMEM((4, width, width), BF16),
                pltpu.SemaphoreType.DMA((depth,)),
                pltpu.SemaphoreType.DMA((4,)),
            ],
            input_output_aliases={} if mixed is None else {7: 0},
            compiler_params=params,
            cost_estimate=cost,
            name="left_mix",
        )(*operands)

    def right_mix(phase, meta):
        keep, send = pl.pallas_call(
            functools.partial(right_kernel, phase),
            out_shape=(
                jax.ShapeDtypeStruct((CORES, half, width), F32),
                jax.ShapeDtypeStruct((bands - 1, CORES, half, width), BF16),
            ),
            in_specs=[SMEM] * 3 + [WHOLE] + [ANY] * 2,
            out_specs=(WHOLE, WHOLE),
            scratch_shapes=[
                pltpu.SMEM((CORES * slots + 1,), jnp.int32),
                pltpu.VMEM((width, width), F32),
                pltpu.VMEM((depth, width, width), BF16),
                pltpu.SemaphoreType.DMA((depth,)),
            ],
            compiler_params=params,
            cost_estimate=cost,
            name="right_mix",
        )(meta, sib_meta, where_dst, mixed, right, right_sib)
        for j in range(1, bands):
            keep = keep + move(send[j - 1], band_step=j).astype(F32)
        return keep

    beside_far = right_mix(0, own_meta).astype(BF16)
    mirrored = right_mix(1, own_meta)
    meta, beside_far = lax.optimization_barrier((own_meta, beside_far))
    mirrored = (mirrored + move(beside_far, beside).astype(F32)).astype(BF16)
    beside_near = right_mix(2, meta).astype(BF16)
    total = right_mix(3, meta) + move(mirrored, mirror).astype(F32) + move(beside_near, beside).astype(F32)
    same, cross = total[0], move(total[1], flip=True)
    first = core == 0
    return jnp.concatenate([jnp.where(first, same, cross), jnp.where(first, cross, same)], axis=1)


def solution(mesh):
    spec = P(("parts", "term"))
    return jax.shard_map(
        functools.partial(local, mesh.shape["term"]),
        mesh=mesh,
        in_specs=(spec,) * 6,
        out_specs=spec,
        check_vma=False,
    )
```

```python
import functools

import jax
import jax.numpy as jnp
from jax import lax
from jax.experimental import pallas as pl
from jax.experimental.pallas import tpu as pltpu
from jax.sharding import PartitionSpec as P

F32, BF16 = jnp.float32, jnp.bfloat16
CORES = 2
VMEM = 24 * 1024 * 1024
ANY = pl.BlockSpec(memory_space=pl.ANY)
SMEM = pl.BlockSpec(memory_space=pltpu.SMEM)
WHOLE = pl.BlockSpec(memory_space=pltpu.VMEM)


def list_slots(own, sib, field, sector, slots, found):
    count = jnp.int32(0)
    for core, meta in enumerate((own, sib)):
        live = meta[2 * slots]
        for t in range(slots):
            found[count] = core * slots + t
            hit = jnp.logical_and(t < live, meta[field * slots + t] == sector)
            count = count + hit.astype(jnp.int32)
    return count


def in_pairs(count, depth, fetch, wait, work):
    for i in range(depth - 2):
        @pl.when(i < count)
        def _():
            fetch(i, i)

    def pair(p, carry):
        i = 2 * p
        for ahead in (i + depth - 2, i + depth - 1):
            @pl.when(ahead < count)
            def _():
                fetch(ahead, lax.rem(ahead, depth))
        spots = [lax.rem(i, depth), lax.rem(i, depth) + 1]
        for k in spots:
            wait(k)
        work((i, i + 1), spots)
        return carry

    lax.fori_loop(0, count // 2, pair, 0)

    @pl.when(count % 2 == 1)
    def _():
        k = lax.rem(count - 1, depth)
        wait(k)
        work((count - 1,), (k,))


def start_fetch(term, slots, own_hbm, sib_hbm, target, sem):
    @pl.when(term < slots)
    def _():
        pltpu.make_async_copy(own_hbm.at[term], target, sem).start()

    @pl.when(term >= slots)
    def _():
        pltpu.make_async_copy(sib_hbm.at[term - slots], target, sem).start()


def left_kernel(phase, *refs):
    (own, sib, where, here, others, left, left_sib), refs = refs[:7], refs[7:]
    mixed, found, source, lbuf, obuf, lsem, osem = refs[-7:]
    slots, depth, outs = left.shape[0], lbuf.shape[0], obuf.shape[0]
    half = here.shape[1]
    bands = others.shape[0] + 1
    sector, band, core = where[phase], where[where.shape[0] - 2], where[where.shape[0] - 1]
    count = list_slots(own, sib, 0, sector, slots, found)

    def fetch(i, k):
        start_fetch(found[i], slots, left, left_sib, lbuf.at[k], lsem.at[k])

    def wait(k):
        pltpu.make_async_copy(left.at[0], lbuf.at[k], lsem.at[k]).wait()

    def out_copy(i, o):
        return pltpu.make_async_copy(obuf.at[o], mixed.at[found[i]], osem.at[o])

    def work(items, spots):
        wide = lbuf.shape[1]
        stack = lbuf[pl.ds(spots[0], len(spots))].reshape(len(spots) * wide, wide)
        product = jnp.dot(stack, source[...], preferred_element_type=F32).astype(BF16)
        for n, i in enumerate(items):
            o = lax.rem(i, outs)

            @pl.when(i >= outs)
            def _():
                out_copy(i - outs, o).wait()

            obuf[o] = product[n * wide : (n + 1) * wide]
            out_copy(i, o).start()

    for j in range(bands):
        b = lax.rem(band + j, bands)
        for i in range(CORES):
            c = core if i == 0 else 1 - core
            row = pl.multiple_of((b * CORES + c) * half, half)
            source[pl.ds(row, half)] = here[i] if j == 0 else others[j - 1, i]
    in_pairs(count, depth, fetch, wait, work)
    for back in range(outs, 0, -1):
        @pl.when(count >= back)
        def _():
            out_copy(count - back, lax.rem(count - back, outs)).wait()


def right_kernel(phase, own, sib, where, mixed, right, right_sib, keep, send, found, acc, rbuf, rsem):
    slots, depth = right.shape[0], rbuf.shape[0]
    half = keep.shape[1]
    bands = send.shape[0] + 1
    sector, band, core = where[phase], where[where.shape[0] - 2], where[where.shape[0] - 1]
    count = list_slots(own, sib, 1, sector, slots, found)

    def fetch(i, k):
        start_fetch(found[i], slots, right, right_sib, rbuf.at[k], rsem.at[k])

    def wait(k):
        pltpu.make_async_copy(right.at[0], rbuf.at[k], rsem.at[k]).wait()

    def work(items, spots):
        lhs = jnp.concatenate([mixed[found[i]] for i in items], axis=1)
        rhs = jnp.concatenate([rbuf[k] for k in spots], axis=1)
        acc[...] += lax.dot_general(lhs, rhs, (((1,), (1,)), ((), ())), preferred_element_type=F32)

    acc[...] = jnp.zeros_like(acc)
    in_pairs(count, depth, fetch, wait, work)
    for j in range(bands):
        b = lax.rem(band + j, bands)
        for i in range(CORES):
            c = core if i == 0 else 1 - core
            rows = acc[pl.ds(pl.multiple_of((b * CORES + c) * half, half), half)]
            if j == 0:
                keep[i] = rows
            else:
                send[j - 1, i] = rows.astype(BF16)


def local(devices, wavefunction, left, right, src, dst, live):
    slots, width = left.shape[0], left.shape[1]
    half = wavefunction.shape[0]
    sectors = half * devices // width
    bands = devices // (sectors * CORES)
    assert sectors == 4
    me = lax.axis_index("term")
    core, band, plane = me % CORES, (me // CORES) % bands, me // (CORES * bands)

    def move(value, to_plane=lambda a: a, band_step=0, flip=False):
        pairs = []
        for i in range(devices):
            c, b, a = i % CORES, (i // CORES) % bands, i // (CORES * bands)
            c = 1 - c if flip else c
            pairs.append((i, (to_plane(a) * bands + (b + band_step) % bands) * CORES + c))
        return lax.ppermute(value, "term", pairs)

    def beside(a):
        return a ^ 1

    def mirror(a):
        return 3 - a

    def bands_of(block):
        return jnp.stack([move(block, band_step=-j) for j in range(1, bands)])

    own_meta = jnp.concatenate([src, dst, live])
    sib_meta = move(own_meta, flip=True)
    mine = lax.dynamic_slice_in_dim(wavefunction, core * width, width, 1)
    theirs = lax.dynamic_slice_in_dim(wavefunction, (1 - core) * width, width, 1)
    from_sib = move(theirs, flip=True)
    left_sib, from_sib, sib_meta = lax.optimization_barrier((left, from_sib, sib_meta))
    left_sib = move(left_sib, flip=True)
    own_block = jnp.stack([mine, from_sib])
    mirror_block = move(own_block, mirror)
    beside_block, own_bands = lax.optimization_barrier((move(own_block, beside), bands_of(own_block)))
    beside_bands = bands_of(beside_block)
    blocks = [(own_block, own_bands), None, None, None]
    partner = plane ^ 1
    where_src = jnp.stack([plane, partner, 3 - plane, 3 - partner, band, core]).astype(jnp.int32)
    where_dst = jnp.stack([3 - partner, 3 - plane, partner, plane, band, core]).astype(jnp.int32)

    params = pltpu.CompilerParams(vmem_limit_bytes=VMEM)
    left_cost = pl.CostEstimate(flops=10**6, bytes_accessed=width, transcendentals=0)
    cost = pl.CostEstimate(flops=3 * 10**9, bytes_accessed=7 * width * width * 2, transcendentals=0)
    depth = 8
    mixed = None
    for phase in range(sectors):
        if phase == 1:
            mirror_block, mixed, right_sib, beside_bands = lax.optimization_barrier(
                (mirror_block, mixed, right, beside_bands)
            )
            right_sib = move(right_sib, flip=True)
            blocks[1] = (beside_block, beside_bands)
            blocks[2] = (mirror_block, bands_of(mirror_block))
            far_block = move(mirror_block, beside)
        if phase == 2:
            far_block, mixed = lax.optimization_barrier((far_block, mixed))
            blocks[3] = (far_block, bands_of(far_block))
        operands = [own_meta, sib_meta, where_src, *blocks[phase], left, left_sib]
        if mixed is not None:
            operands.append(mixed)
        mixed = pl.pallas_call(
            functools.partial(left_kernel, phase),
            out_shape=jax.ShapeDtypeStruct((CORES * slots, width, width), BF16),
            in_specs=[SMEM] * 3 + [WHOLE] * 2 + [ANY] * (len(operands) - 5),
            out_specs=ANY,
            scratch_shapes=[
                pltpu.SMEM((CORES * slots + 1,), jnp.int32),
                pltpu.VMEM((width, width), BF16),
                pltpu.VMEM((depth, width, width), BF16),
                pltpu.VMEM((4, width, width), BF16),
                pltpu.SemaphoreType.DMA((depth,)),
                pltpu.SemaphoreType.DMA((4,)),
            ],
            input_output_aliases={} if mixed is None else {7: 0},
            compiler_params=params,
            cost_estimate=left_cost,
            name="left_mix",
        )(*operands)

    def right_mix(phase, meta):
        keep, send = pl.pallas_call(
            functools.partial(right_kernel, phase),
            out_shape=(
                jax.ShapeDtypeStruct((CORES, half, width), F32),
                jax.ShapeDtypeStruct((bands - 1, CORES, half, width), BF16),
            ),
            in_specs=[SMEM] * 3 + [WHOLE] + [ANY] * 2,
            out_specs=(WHOLE, WHOLE),
            scratch_shapes=[
                pltpu.SMEM((CORES * slots + 1,), jnp.int32),
                pltpu.VMEM((width, width), F32),
                pltpu.VMEM((depth, width, width), BF16),
                pltpu.SemaphoreType.DMA((depth,)),
            ],
            compiler_params=params,
            cost_estimate=cost,
            name="right_mix",
        )(meta, sib_meta, where_dst, mixed, right, right_sib)
        for j in range(1, bands):
            keep = keep + move(send[j - 1], band_step=j).astype(F32)
        return keep

    beside_far = right_mix(0, own_meta).astype(BF16)
    mirrored = right_mix(1, own_meta)
    meta, beside_far = lax.optimization_barrier((own_meta, beside_far))
    mirrored = (mirrored + move(beside_far, beside).astype(F32)).astype(BF16)
    beside_near = right_mix(2, meta).astype(BF16)
    meta, mirrored = lax.optimization_barrier((meta, mirrored))
    total = right_mix(3, meta) + move(mirrored, mirror).astype(F32) + move(beside_near, beside).astype(F32)
    same, cross = total[0], move(total[1], flip=True)
    first = core == 0
    return jnp.concatenate([jnp.where(first, same, cross), jnp.where(first, cross, same)], axis=1)


def solution(mesh):
    spec = P(("parts", "term"))
    return jax.shard_map(
        functools.partial(local, mesh.shape["term"]),
        mesh=mesh,
        in_specs=(spec,) * 6,
        out_specs=spec,
        check_vma=False,
    )
```

```python
import functools

import jax
import jax.numpy as jnp
from jax import lax
from jax.experimental import pallas as pl
from jax.experimental.pallas import tpu as pltpu
from jax.sharding import PartitionSpec as P

F32, BF16 = jnp.float32, jnp.bfloat16
CORES = 2
TILE = 256
VMEM = 16 * 1024 * 1024
ANY = pl.BlockSpec(memory_space=pl.ANY)
SMEM = pl.BlockSpec(memory_space=pltpu.SMEM)
WHOLE = pl.BlockSpec(memory_space=pltpu.VMEM)


def list_slots(own, sib, field, sector, slots, found):
    count = jnp.int32(0)
    for core, meta in enumerate((own, sib)):
        live = meta[2 * slots]
        for t in range(slots):
            found[count] = core * slots + t
            hit = jnp.logical_and(t < live, meta[field * slots + t] == sector)
            count = count + hit.astype(jnp.int32)
    return count


def in_pairs(count, depth, fetch, wait, work):
    for i in range(depth - 2):
        @pl.when(i < count)
        def _():
            fetch(i, i)

    def pair(p, carry):
        i = 2 * p
        for ahead in (i + depth - 2, i + depth - 1):
            @pl.when(ahead < count)
            def _():
                fetch(ahead, lax.rem(ahead, depth))
        spots = [lax.rem(i, depth), lax.rem(i, depth) + 1]
        for k in spots:
            wait(k)
        work((i, i + 1), spots)
        return carry

    lax.fori_loop(0, count // 2, pair, 0)

    @pl.when(count % 2 == 1)
    def _():
        k = lax.rem(count - 1, depth)
        wait(k)
        work((count - 1,), (k,))


def start_fetch(term, slots, own_hbm, sib_hbm, target, sem):
    @pl.when(term < slots)
    def _():
        pltpu.make_async_copy(own_hbm.at[term], target, sem).start()

    @pl.when(term >= slots)
    def _():
        pltpu.make_async_copy(sib_hbm.at[term - slots], target, sem).start()


def left_kernel(phase, *refs):
    (own, sib, where, here, others, left, left_sib), refs = refs[:7], refs[7:]
    mixed, token, found, source, lbuf, obuf, lsem, osem = refs[-8:]
    token[...] = jnp.zeros_like(token)
    slots, depth, outs = left.shape[0], lbuf.shape[0], obuf.shape[0]
    half = here.shape[1]
    bands = others.shape[0] + 1
    sector, band, core = where[phase], where[where.shape[0] - 2], where[where.shape[0] - 1]
    count = list_slots(own, sib, 0, sector, slots, found)

    def fetch(i, k):
        start_fetch(found[i], slots, left, left_sib, lbuf.at[k], lsem.at[k])

    def wait(k):
        pltpu.make_async_copy(left.at[0], lbuf.at[k], lsem.at[k]).wait()

    def out_copy(i, o):
        return pltpu.make_async_copy(obuf.at[o], mixed.at[found[i]], osem.at[o])

    def work(items, spots):
        for i, k in zip(items, spots):
            o = lax.rem(i, outs)

            @pl.when(i >= outs)
            def _():
                out_copy(i - outs, o).wait()

            for n in range(0, source.shape[1], TILE):
                for m in range(0, source.shape[0], TILE):
                    obuf[o, m : m + TILE, n : n + TILE] = jnp.dot(
                        lbuf[k, m : m + TILE, :], source[:, n : n + TILE], preferred_element_type=F32
                    ).astype(BF16)
            out_copy(i, o).start()

    for j in range(bands):
        b = lax.rem(band + j, bands)
        for i in range(CORES):
            c = core if i == 0 else 1 - core
            row = pl.multiple_of((b * CORES + c) * half, half)
            source[pl.ds(row, half)] = here[i] if j == 0 else others[j - 1, i]
    in_pairs(count, depth, fetch, wait, work)
    for back in range(outs, 0, -1):
        @pl.when(count >= back)
        def _():
            out_copy(count - back, lax.rem(count - back, outs)).wait()


def right_kernel(phase, own, sib, where, mixed, right, right_sib, keep, send, found, acc, rbuf, rsem):
    slots, depth = right.shape[0], rbuf.shape[0]
    half = keep.shape[1]
    bands = send.shape[0] + 1
    sector, band, core = where[phase], where[where.shape[0] - 2], where[where.shape[0] - 1]
    count = list_slots(own, sib, 1, sector, slots, found)

    def fetch(i, k):
        start_fetch(found[i], slots, right, right_sib, rbuf.at[k], rsem.at[k])

    def wait(k):
        pltpu.make_async_copy(right.at[0], rbuf.at[k], rsem.at[k]).wait()

    def work(items, spots):
        for n in range(0, acc.shape[1], TILE):
            acc[:, n : n + TILE] += sum(
                lax.dot_general(
                    mixed[found[i]], rbuf[k, n : n + TILE, :], (((1,), (1,)), ((), ())), preferred_element_type=F32
                )
                for i, k in zip(items, spots)
            )

    acc[...] = jnp.zeros_like(acc)
    in_pairs(count, depth, fetch, wait, work)
    for j in range(bands):
        b = lax.rem(band + j, bands)
        for i in range(CORES):
            c = core if i == 0 else 1 - core
            rows = acc[pl.ds(pl.multiple_of((b * CORES + c) * half, half), half)]
            if j == 0:
                keep[i] = rows
            else:
                send[j - 1, i] = rows.astype(BF16)


def local(devices, wavefunction, left, right, src, dst, live):
    slots, width = left.shape[0], left.shape[1]
    half = wavefunction.shape[0]
    sectors = half * devices // width
    bands = devices // (sectors * CORES)
    assert sectors == 4
    me = lax.axis_index("term")
    core, band, plane = me % CORES, (me // CORES) % bands, me // (CORES * bands)

    def move(value, to_plane=lambda a: a, band_step=0, flip=False):
        pairs = []
        for i in range(devices):
            c, b, a = i % CORES, (i // CORES) % bands, i // (CORES * bands)
            c = 1 - c if flip else c
            pairs.append((i, (to_plane(a) * bands + (b + band_step) % bands) * CORES + c))
        return lax.ppermute(value, "term", pairs)

    def beside(a):
        return a ^ 1

    def mirror(a):
        return 3 - a

    def bands_of(block):
        return jnp.stack([move(block, band_step=-j) for j in range(1, bands)])

    own_meta = jnp.concatenate([src, dst, live])
    sib_meta = move(own_meta, flip=True)
    mine = lax.dynamic_slice_in_dim(wavefunction, core * width, width, 1)
    theirs = lax.dynamic_slice_in_dim(wavefunction, (1 - core) * width, width, 1)
    from_sib = move(theirs, flip=True)
    left_sib, from_sib, sib_meta = lax.optimization_barrier((left, from_sib, sib_meta))
    left_sib = move(left_sib, flip=True)
    own_block = jnp.stack([mine, from_sib])
    mirror_block = move(own_block, mirror)
    beside_block, own_bands = lax.optimization_barrier((move(own_block, beside), bands_of(own_block)))
    beside_bands = bands_of(beside_block)
    blocks = [(own_block, own_bands), None, None, None]
    partner = plane ^ 1
    where_src = jnp.stack([plane, partner, 3 - plane, 3 - partner, band, core]).astype(jnp.int32)
    where_dst = jnp.stack([3 - partner, 3 - plane, partner, plane, band, core]).astype(jnp.int32)

    params = pltpu.CompilerParams(vmem_limit_bytes=VMEM)
    left_cost = pl.CostEstimate(flops=10**6, bytes_accessed=width, transcendentals=0)
    cost = pl.CostEstimate(flops=3 * 10**9, bytes_accessed=7 * width * width * 2, transcendentals=0)
    depth = 8
    mixed = None
    for phase in range(sectors):
        if phase == 1:
            mirror_block, right_sib, beside_bands, token = lax.optimization_barrier(
                (mirror_block, right, beside_bands, token)
            )
            right_sib = move(right_sib, flip=True)
            blocks[1] = (beside_block, beside_bands)
            blocks[2] = (mirror_block, bands_of(mirror_block))
            far_block = move(mirror_block, beside)
        if phase == 2:
            far_block, token = lax.optimization_barrier((far_block, token))
            blocks[3] = (far_block, bands_of(far_block))
        operands = [own_meta, sib_meta, where_src, *blocks[phase], left, left_sib]
        if mixed is not None:
            operands += [mixed, token]
        mixed, token = pl.pallas_call(
            functools.partial(left_kernel, phase),
            out_shape=(
                jax.ShapeDtypeStruct((CORES * slots, width, width), BF16),
                jax.ShapeDtypeStruct((8, 128), F32),
            ),
            in_specs=[SMEM] * 3 + [WHOLE] * 2 + [ANY] * (len(operands) - 5),
            out_specs=(ANY, WHOLE),
            scratch_shapes=[
                pltpu.SMEM((CORES * slots + 1,), jnp.int32),
                pltpu.VMEM((width, width), BF16),
                pltpu.VMEM((depth, width, width), BF16),
                pltpu.VMEM((4, width, width), BF16),
                pltpu.SemaphoreType.DMA((depth,)),
                pltpu.SemaphoreType.DMA((4,)),
            ],
            input_output_aliases={} if mixed is None else {7: 0},
            compiler_params=params,
            cost_estimate=left_cost,
            name="left_mix",
        )(*operands)

    def right_mix(phase, meta):
        keep, send = pl.pallas_call(
            functools.partial(right_kernel, phase),
            out_shape=(
                jax.ShapeDtypeStruct((CORES, half, width), F32),
                jax.ShapeDtypeStruct((bands - 1, CORES, half, width), BF16),
            ),
            in_specs=[SMEM] * 3 + [WHOLE] + [ANY] * 2,
            out_specs=(WHOLE, WHOLE),
            scratch_shapes=[
                pltpu.SMEM((CORES * slots + 1,), jnp.int32),
                pltpu.VMEM((width, width), F32),
                pltpu.VMEM((depth, width, width), BF16),
                pltpu.SemaphoreType.DMA((depth,)),
            ],
            compiler_params=params,
            cost_estimate=cost,
            name="right_mix",
        )(meta, sib_meta, where_dst, mixed, right, right_sib)
        for j in range(1, bands):
            keep = keep + move(send[j - 1], band_step=j).astype(F32)
        return keep

    beside_far = right_mix(0, own_meta).astype(BF16)
    mirrored = right_mix(1, own_meta)
    meta, beside_far = lax.optimization_barrier((own_meta, beside_far))
    mirrored = (mirrored + move(beside_far, beside).astype(F32)).astype(BF16)
    beside_near = right_mix(2, meta).astype(BF16)
    total = right_mix(3, meta) + move(mirrored, mirror).astype(F32) + move(beside_near, beside).astype(F32)
    same, cross = total[0], move(total[1], flip=True)
    first = core == 0
    return jnp.concatenate([jnp.where(first, same, cross), jnp.where(first, cross, same)], axis=1)


def solution(mesh):
    spec = P(("parts", "term"))
    return jax.shard_map(
        functools.partial(local, mesh.shape["term"]),
        mesh=mesh,
        in_specs=(spec,) * 6,
        out_specs=spec,
        check_vma=False,
    )
```

```python
import functools

import jax
import jax.numpy as jnp
from jax import lax
from jax.experimental import pallas as pl
from jax.experimental.pallas import tpu as pltpu
from jax.sharding import PartitionSpec as P

F32, BF16 = jnp.float32, jnp.bfloat16
CORES = 2
TILE = 256
VMEM = 48 * 1024 * 1024
ANY = pl.BlockSpec(memory_space=pl.ANY)
SMEM = pl.BlockSpec(memory_space=pltpu.SMEM)
WHOLE = pl.BlockSpec(memory_space=pltpu.VMEM)


def list_slots(own, sib, field, sector, slots, found):
    count = jnp.int32(0)
    for core, meta in enumerate((own, sib)):
        live = meta[2 * slots]
        for t in range(slots):
            found[count] = core * slots + t
            hit = jnp.logical_and(t < live, meta[field * slots + t] == sector)
            count = count + hit.astype(jnp.int32)
    return count


def in_pairs(count, depth, fetch, wait, work):
    for i in range(depth - 2):
        @pl.when(i < count)
        def _():
            fetch(i, i)

    def pair(p, carry):
        i = 2 * p
        for ahead in (i + depth - 2, i + depth - 1):
            @pl.when(ahead < count)
            def _():
                fetch(ahead, lax.rem(ahead, depth))
        spots = [lax.rem(i, depth), lax.rem(i, depth) + 1]
        for k in spots:
            wait(k)
        work((i, i + 1), spots)
        return carry

    lax.fori_loop(0, count // 2, pair, 0)

    @pl.when(count % 2 == 1)
    def _():
        k = lax.rem(count - 1, depth)
        wait(k)
        work((count - 1,), (k,))


def start_fetch(term, slots, own_hbm, sib_hbm, target, sem):
    @pl.when(term < slots)
    def _():
        pltpu.make_async_copy(own_hbm.at[term], target, sem).start()

    @pl.when(term >= slots)
    def _():
        pltpu.make_async_copy(sib_hbm.at[term - slots], target, sem).start()


def left_kernel(phase, *refs):
    (own, sib, where, here, others, left, left_sib), refs = refs[:7], refs[7:]
    mixed, token, found, source, lbuf, obuf, lsem, osem = refs[-8:]
    token[...] = jnp.zeros_like(token)
    slots, depth, outs = left.shape[0], lbuf.shape[0], obuf.shape[0]
    half = here.shape[1]
    bands = others.shape[0] + 1
    sector, band, core = where[phase], where[where.shape[0] - 2], where[where.shape[0] - 1]
    count = list_slots(own, sib, 0, sector, slots, found)

    def fetch(i, k):
        start_fetch(found[i], slots, left, left_sib, lbuf.at[k], lsem.at[k])

    def wait(k):
        pltpu.make_async_copy(left.at[0], lbuf.at[k], lsem.at[k]).wait()

    def out_copy(i, o):
        return pltpu.make_async_copy(obuf.at[o], mixed.at[found[i]], osem.at[o])

    def work(items, spots):
        for i, k in zip(items, spots):
            o = lax.rem(i, outs)

            @pl.when(i >= outs)
            def _():
                out_copy(i - outs, o).wait()

            for n in range(0, source.shape[1], TILE):
                for m in range(0, source.shape[0], TILE):
                    obuf[o, m : m + TILE, n : n + TILE] = jnp.dot(
                        lbuf[k, m : m + TILE, :], source[:, n : n + TILE], preferred_element_type=F32
                    ).astype(BF16)
            out_copy(i, o).start()

    for j in range(bands):
        b = lax.rem(band + j, bands)
        for i in range(CORES):
            c = core if i == 0 else 1 - core
            row = pl.multiple_of((b * CORES + c) * half, half)
            source[pl.ds(row, half)] = here[i] if j == 0 else others[j - 1, i]
    in_pairs(count, depth, fetch, wait, work)
    for back in range(outs, 0, -1):
        @pl.when(count >= back)
        def _():
            out_copy(count - back, lax.rem(count - back, outs)).wait()


def right_kernel(phase, own, sib, where, mixed, right, right_sib, keep, send, found, acc, rbuf, rsem):
    slots, depth = right.shape[0], rbuf.shape[0]
    half = keep.shape[1]
    bands = send.shape[0] + 1
    sector, band, core = where[phase], where[where.shape[0] - 2], where[where.shape[0] - 1]
    count = list_slots(own, sib, 1, sector, slots, found)

    def fetch(i, k):
        start_fetch(found[i], slots, right, right_sib, rbuf.at[k], rsem.at[k])

    def wait(k):
        pltpu.make_async_copy(right.at[0], rbuf.at[k], rsem.at[k]).wait()

    def work(items, spots):
        for n in range(0, acc.shape[1], TILE):
            acc[:, n : n + TILE] += sum(
                lax.dot_general(
                    mixed[found[i]], rbuf[k, n : n + TILE, :], (((1,), (1,)), ((), ())), preferred_element_type=F32
                )
                for i, k in zip(items, spots)
            )

    acc[...] = jnp.zeros_like(acc)
    in_pairs(count, depth, fetch, wait, work)
    for j in range(bands):
        b = lax.rem(band + j, bands)
        for i in range(CORES):
            c = core if i == 0 else 1 - core
            rows = acc[pl.ds(pl.multiple_of((b * CORES + c) * half, half), half)]
            if j == 0:
                keep[i] = rows
            else:
                send[j - 1, i] = rows.astype(BF16)


def local(devices, wavefunction, left, right, src, dst, live):
    slots, width = left.shape[0], left.shape[1]
    half = wavefunction.shape[0]
    sectors = half * devices // width
    bands = devices // (sectors * CORES)
    assert sectors == 4
    me = lax.axis_index("term")
    core, band, plane = me % CORES, (me // CORES) % bands, me // (CORES * bands)

    def move(value, to_plane=lambda a: a, band_step=0, flip=False):
        pairs = []
        for i in range(devices):
            c, b, a = i % CORES, (i // CORES) % bands, i // (CORES * bands)
            c = 1 - c if flip else c
            pairs.append((i, (to_plane(a) * bands + (b + band_step) % bands) * CORES + c))
        return lax.ppermute(value, "term", pairs)

    def beside(a):
        return a ^ 1

    def mirror(a):
        return 3 - a

    def bands_of(block):
        return jnp.stack([move(block, band_step=-j) for j in range(1, bands)])

    own_meta = jnp.concatenate([src, dst, live])
    sib_meta = move(own_meta, flip=True)
    mine = lax.dynamic_slice_in_dim(wavefunction, core * width, width, 1)
    theirs = lax.dynamic_slice_in_dim(wavefunction, (1 - core) * width, width, 1)
    from_sib = move(theirs, flip=True)
    left_sib, from_sib, sib_meta = lax.optimization_barrier((left, from_sib, sib_meta))
    left_sib = move(left_sib, flip=True)
    own_block = jnp.stack([mine, from_sib])
    mirror_block = move(own_block, mirror)
    beside_block, own_bands = lax.optimization_barrier((move(own_block, beside), bands_of(own_block)))
    beside_bands = bands_of(beside_block)
    blocks = [(own_block, own_bands), None, None, None]
    partner = plane ^ 1
    where_src = jnp.stack([plane, partner, 3 - plane, 3 - partner, band, core]).astype(jnp.int32)
    where_dst = jnp.stack([3 - partner, 3 - plane, partner, plane, band, core]).astype(jnp.int32)

    params = pltpu.CompilerParams(vmem_limit_bytes=VMEM)
    left_cost = pl.CostEstimate(flops=10**6, bytes_accessed=width, transcendentals=0)
    cost = pl.CostEstimate(flops=3 * 10**9, bytes_accessed=7 * width * width * 2, transcendentals=0)
    depth = 8
    mixed = None
    for phase in range(sectors):
        if phase == 1:
            mirror_block, right_sib, beside_bands, token = lax.optimization_barrier(
                (mirror_block, right, beside_bands, token)
            )
            right_sib = move(right_sib, flip=True)
            blocks[1] = (beside_block, beside_bands)
            blocks[2] = (mirror_block, bands_of(mirror_block))
            far_block = move(mirror_block, beside)
        if phase == 2:
            far_block, token = lax.optimization_barrier((far_block, token))
            blocks[3] = (far_block, bands_of(far_block))
        operands = [own_meta, sib_meta, where_src, *blocks[phase], left, left_sib]
        if mixed is not None:
            operands += [mixed, token]
        mixed, token = pl.pallas_call(
            functools.partial(left_kernel, phase),
            out_shape=(
                jax.ShapeDtypeStruct((CORES * slots, width, width), BF16),
                jax.ShapeDtypeStruct((8, 128), F32),
            ),
            in_specs=[SMEM] * 3 + [WHOLE] * 2 + [ANY] * (len(operands) - 5),
            out_specs=(ANY, WHOLE),
            scratch_shapes=[
                pltpu.SMEM((CORES * slots + 1,), jnp.int32),
                pltpu.VMEM((width, width), BF16),
                pltpu.VMEM((depth, width, width), BF16),
                pltpu.VMEM((4, width, width), BF16),
                pltpu.SemaphoreType.DMA((depth,)),
                pltpu.SemaphoreType.DMA((4,)),
            ],
            input_output_aliases={} if mixed is None else {7: 0},
            compiler_params=params,
            cost_estimate=left_cost,
            name="left_mix",
        )(*operands)

    def right_mix(phase, meta):
        keep, send = pl.pallas_call(
            functools.partial(right_kernel, phase),
            out_shape=(
                jax.ShapeDtypeStruct((CORES, half, width), F32),
                jax.ShapeDtypeStruct((bands - 1, CORES, half, width), BF16),
            ),
            in_specs=[SMEM] * 3 + [WHOLE] + [ANY] * 2,
            out_specs=(WHOLE, WHOLE),
            scratch_shapes=[
                pltpu.SMEM((CORES * slots + 1,), jnp.int32),
                pltpu.VMEM((width, width), F32),
                pltpu.VMEM((depth, width, width), BF16),
                pltpu.SemaphoreType.DMA((depth,)),
            ],
            compiler_params=params,
            cost_estimate=cost,
            name="right_mix",
        )(meta, sib_meta, where_dst, mixed, right, right_sib)
        for j in range(1, bands):
            keep = keep + move(send[j - 1], band_step=j).astype(F32)
        return keep

    beside_far = right_mix(0, own_meta).astype(BF16)
    mirrored = right_mix(1, own_meta)
    meta, beside_far = lax.optimization_barrier((own_meta, beside_far))
    mirrored = (mirrored + move(beside_far, beside).astype(F32)).astype(BF16)
    beside_near = right_mix(2, meta).astype(BF16)
    total = right_mix(3, meta) + move(mirrored, mirror).astype(F32) + move(beside_near, beside).astype(F32)
    same, cross = total[0], move(total[1], flip=True)
    first = core == 0
    return jnp.concatenate([jnp.where(first, same, cross), jnp.where(first, cross, same)], axis=1)


def solution(mesh):
    spec = P(("parts", "term"))
    return jax.shard_map(
        functools.partial(local, mesh.shape["term"]),
        mesh=mesh,
        in_specs=(spec,) * 6,
        out_specs=spec,
        check_vma=False,
    )
```

```python
import functools

import jax
import jax.numpy as jnp
from jax import lax
from jax.experimental import pallas as pl
from jax.experimental.pallas import tpu as pltpu
from jax.sharding import PartitionSpec as P

F32, BF16 = jnp.float32, jnp.bfloat16
CORES = 2
VMEM = 48 * 1024 * 1024
ANY = pl.BlockSpec(memory_space=pl.ANY)
SMEM = pl.BlockSpec(memory_space=pltpu.SMEM)
WHOLE = pl.BlockSpec(memory_space=pltpu.VMEM)


def list_slots(own, sib, field, sector, slots, found):
    count = jnp.int32(0)
    for core, meta in enumerate((own, sib)):
        live = meta[2 * slots]
        for t in range(slots):
            found[count] = core * slots + t
            hit = jnp.logical_and(t < live, meta[field * slots + t] == sector)
            count = count + hit.astype(jnp.int32)
    return count


def in_pairs(count, depth, fetch, wait, work):
    for i in range(depth - 2):
        @pl.when(i < count)
        def _():
            fetch(i, i)

    def pair(p, carry):
        i = 2 * p
        for ahead in (i + depth - 2, i + depth - 1):
            @pl.when(ahead < count)
            def _():
                fetch(ahead, lax.rem(ahead, depth))
        spots = [lax.rem(i, depth), lax.rem(i, depth) + 1]
        for k in spots:
            wait(k)
        work((i, i + 1), spots)
        return carry

    lax.fori_loop(0, count // 2, pair, 0)

    @pl.when(count % 2 == 1)
    def _():
        k = lax.rem(count - 1, depth)
        wait(k)
        work((count - 1,), (k,))


def start_fetch(term, slots, own_hbm, sib_hbm, target, sem):
    @pl.when(term < slots)
    def _():
        pltpu.make_async_copy(own_hbm.at[term], target, sem).start()

    @pl.when(term >= slots)
    def _():
        pltpu.make_async_copy(sib_hbm.at[term - slots], target, sem).start()


def left_kernel(phase, *refs):
    (own, sib, where, here, others, left, left_sib), refs = refs[:7], refs[7:]
    mixed, token, found, source, lbuf, obuf, lsem, osem = refs[-8:]
    token[...] = jnp.zeros_like(token)
    slots, depth, outs = left.shape[0], lbuf.shape[0], obuf.shape[0]
    half = here.shape[1]
    bands = others.shape[0] + 1
    sector, band, core = where[phase], where[where.shape[0] - 2], where[where.shape[0] - 1]
    count = list_slots(own, sib, 0, sector, slots, found)

    def fetch(i, k):
        start_fetch(found[i], slots, left, left_sib, lbuf.at[k], lsem.at[k])

    def wait(k):
        pltpu.make_async_copy(left.at[0], lbuf.at[k], lsem.at[k]).wait()

    def out_copy(i, o):
        return pltpu.make_async_copy(obuf.at[o], mixed.at[found[i]], osem.at[o])

    def work(items, spots):
        for i, k in zip(items, spots):
            o = lax.rem(i, outs)

            @pl.when(i >= outs)
            def _():
                out_copy(i - outs, o).wait()

            obuf[o] = jnp.dot(lbuf[k], source[...], preferred_element_type=F32).astype(BF16)
            out_copy(i, o).start()

    for j in range(bands):
        b = lax.rem(band + j, bands)
        for i in range(CORES):
            c = core if i == 0 else 1 - core
            row = pl.multiple_of((b * CORES + c) * half, half)
            source[pl.ds(row, half)] = here[i] if j == 0 else others[j - 1, i]
    in_pairs(count, depth, fetch, wait, work)
    for back in range(outs, 0, -1):
        @pl.when(count >= back)
        def _():
            out_copy(count - back, lax.rem(count - back, outs)).wait()


def right_kernel(phase, *refs):
    own, sib, where, mixed, right, right_sib, keep, send, found, acc, mbuf, rbuf, msem, rsem = refs
    slots, depth = right.shape[0], rbuf.shape[0]
    half = keep.shape[1]
    bands = send.shape[0] + 1
    sector, band, core = where[phase], where[where.shape[0] - 2], where[where.shape[0] - 1]
    count = list_slots(own, sib, 1, sector, slots, found)

    def fetch(i, k):
        pltpu.make_async_copy(mixed.at[found[i]], mbuf.at[k], msem.at[k]).start()
        start_fetch(found[i], slots, right, right_sib, rbuf.at[k], rsem.at[k])

    def wait(k):
        pltpu.make_async_copy(mixed.at[0], mbuf.at[k], msem.at[k]).wait()
        pltpu.make_async_copy(right.at[0], rbuf.at[k], rsem.at[k]).wait()

    def work(items, spots):
        acc[...] += sum(
            lax.dot_general(mbuf[k], rbuf[k], (((1,), (1,)), ((), ())), preferred_element_type=F32) for k in spots
        )

    acc[...] = jnp.zeros_like(acc)
    in_pairs(count, depth, fetch, wait, work)
    for j in range(bands):
        b = lax.rem(band + j, bands)
        for i in range(CORES):
            c = core if i == 0 else 1 - core
            rows = acc[pl.ds(pl.multiple_of((b * CORES + c) * half, half), half)]
            if j == 0:
                keep[i] = rows
            else:
                send[j - 1, i] = rows.astype(BF16)


def local(devices, wavefunction, left, right, src, dst, live):
    slots, width = left.shape[0], left.shape[1]
    half = wavefunction.shape[0]
    sectors = half * devices // width
    bands = devices // (sectors * CORES)
    assert sectors == 4
    me = lax.axis_index("term")
    core, band, plane = me % CORES, (me // CORES) % bands, me // (CORES * bands)

    def move(value, to_plane=lambda a: a, band_step=0, flip=False):
        pairs = []
        for i in range(devices):
            c, b, a = i % CORES, (i // CORES) % bands, i // (CORES * bands)
            c = 1 - c if flip else c
            pairs.append((i, (to_plane(a) * bands + (b + band_step) % bands) * CORES + c))
        return lax.ppermute(value, "term", pairs)

    def beside(a):
        return a ^ 1

    def mirror(a):
        return 3 - a

    def bands_of(block):
        return jnp.stack([move(block, band_step=-j) for j in range(1, bands)])

    own_meta = jnp.concatenate([src, dst, live])
    sib_meta = move(own_meta, flip=True)
    mine = lax.dynamic_slice_in_dim(wavefunction, core * width, width, 1)
    theirs = lax.dynamic_slice_in_dim(wavefunction, (1 - core) * width, width, 1)
    from_sib = move(theirs, flip=True)
    left_sib, from_sib, sib_meta = lax.optimization_barrier((left, from_sib, sib_meta))
    left_sib = move(left_sib, flip=True)
    own_block = jnp.stack([mine, from_sib])
    mirror_block = move(own_block, mirror)
    beside_block, own_bands = lax.optimization_barrier((move(own_block, beside), bands_of(own_block)))
    beside_bands = bands_of(beside_block)
    blocks = [(own_block, own_bands), None, None, None]
    partner = plane ^ 1
    where_src = jnp.stack([plane, partner, 3 - plane, 3 - partner, band, core]).astype(jnp.int32)
    where_dst = jnp.stack([3 - partner, 3 - plane, partner, plane, band, core]).astype(jnp.int32)

    params = pltpu.CompilerParams(vmem_limit_bytes=VMEM)
    left_cost = pl.CostEstimate(flops=10**6, bytes_accessed=width, transcendentals=0)
    cost = pl.CostEstimate(flops=3 * 10**9, bytes_accessed=7 * width * width * 2, transcendentals=0)
    depth = 8
    mixed = None
    for phase in range(sectors):
        if phase == 1:
            mirror_block, right_sib, beside_bands, token = lax.optimization_barrier(
                (mirror_block, right, beside_bands, token)
            )
            right_sib = move(right_sib, flip=True)
            blocks[1] = (beside_block, beside_bands)
            blocks[2] = (mirror_block, bands_of(mirror_block))
            far_block = move(mirror_block, beside)
        if phase == 2:
            far_block, token = lax.optimization_barrier((far_block, token))
            blocks[3] = (far_block, bands_of(far_block))
        operands = [own_meta, sib_meta, where_src, *blocks[phase], left, left_sib]
        if mixed is not None:
            operands += [mixed, token]
        mixed, token = pl.pallas_call(
            functools.partial(left_kernel, phase),
            out_shape=(
                jax.ShapeDtypeStruct((CORES * slots, width, width), BF16),
                jax.ShapeDtypeStruct((8, 128), F32),
            ),
            in_specs=[SMEM] * 3 + [WHOLE] * 2 + [ANY] * (len(operands) - 5),
            out_specs=(ANY, WHOLE),
            scratch_shapes=[
                pltpu.SMEM((CORES * slots + 1,), jnp.int32),
                pltpu.VMEM((width, width), BF16),
                pltpu.VMEM((depth, width, width), BF16),
                pltpu.VMEM((4, width, width), BF16),
                pltpu.SemaphoreType.DMA((depth,)),
                pltpu.SemaphoreType.DMA((4,)),
            ],
            input_output_aliases={} if mixed is None else {7: 0},
            compiler_params=params,
            cost_estimate=left_cost,
            name="left_mix",
        )(*operands)

    def right_mix(phase, meta):
        keep, send = pl.pallas_call(
            functools.partial(right_kernel, phase),
            out_shape=(
                jax.ShapeDtypeStruct((CORES, half, width), F32),
                jax.ShapeDtypeStruct((bands - 1, CORES, half, width), BF16),
            ),
            in_specs=[SMEM] * 3 + [ANY] * 3,
            out_specs=(WHOLE, WHOLE),
            scratch_shapes=[
                pltpu.SMEM((CORES * slots + 1,), jnp.int32),
                pltpu.VMEM((width, width), F32),
                pltpu.VMEM((depth, width, width), BF16),
                pltpu.VMEM((depth, width, width), BF16),
                pltpu.SemaphoreType.DMA((depth,)),
                pltpu.SemaphoreType.DMA((depth,)),
            ],
            compiler_params=params,
            cost_estimate=cost,
            name="right_mix",
        )(meta, sib_meta, where_dst, mixed, right, right_sib)
        for j in range(1, bands):
            keep = keep + move(send[j - 1], band_step=j).astype(F32)
        return keep

    beside_far = right_mix(0, own_meta).astype(BF16)
    mirrored = right_mix(1, own_meta)
    meta, beside_far = lax.optimization_barrier((own_meta, beside_far))
    mirrored = (mirrored + move(beside_far, beside).astype(F32)).astype(BF16)
    beside_near = right_mix(2, meta).astype(BF16)
    total = right_mix(3, meta) + move(mirrored, mirror).astype(F32) + move(beside_near, beside).astype(F32)
    same, cross = total[0], move(total[1], flip=True)
    first = core == 0
    return jnp.concatenate([jnp.where(first, same, cross), jnp.where(first, cross, same)], axis=1)


def solution(mesh):
    spec = P(("parts", "term"))
    return jax.shard_map(
        functools.partial(local, mesh.shape["term"]),
        mesh=mesh,
        in_specs=(spec,) * 6,
        out_specs=spec,
        check_vma=False,
    )
```

```python
import functools

import jax
import jax.numpy as jnp
from jax import lax
from jax.experimental import pallas as pl
from jax.experimental.pallas import tpu as pltpu
from jax.sharding import PartitionSpec as P

F32, BF16 = jnp.float32, jnp.bfloat16
CORES = 2
VMEM = 16 * 1024 * 1024
ANY = pl.BlockSpec(memory_space=pl.ANY)
SMEM = pl.BlockSpec(memory_space=pltpu.SMEM)
WHOLE = pl.BlockSpec(memory_space=pltpu.VMEM)


def list_slots(own, sib, field, sector, slots, found):
    count = jnp.int32(0)
    for core, meta in enumerate((own, sib)):
        live = meta[2 * slots]
        for t in range(slots):
            found[count] = core * slots + t
            hit = jnp.logical_and(t < live, meta[field * slots + t] == sector)
            count = count + hit.astype(jnp.int32)
    return count


def in_pairs(count, depth, fetch, wait, work):
    for i in range(depth - 2):
        @pl.when(i < count)
        def _():
            fetch(i, i)

    def pair(p, carry):
        i = 2 * p
        for ahead in (i + depth - 2, i + depth - 1):
            @pl.when(ahead < count)
            def _():
                fetch(ahead, lax.rem(ahead, depth))
        spots = [lax.rem(i, depth), lax.rem(i, depth) + 1]
        for k in spots:
            wait(k)
        work((i, i + 1), spots)
        return carry

    lax.fori_loop(0, count // 2, pair, 0)

    @pl.when(count % 2 == 1)
    def _():
        k = lax.rem(count - 1, depth)
        wait(k)
        work((count - 1,), (k,))


def start_fetch(term, slots, own_hbm, sib_hbm, target, sem):
    @pl.when(term < slots)
    def _():
        pltpu.make_async_copy(own_hbm.at[term], target, sem).start()

    @pl.when(term >= slots)
    def _():
        pltpu.make_async_copy(sib_hbm.at[term - slots], target, sem).start()


def left_kernel(phase, *refs):
    (own, sib, where, here, others, left, left_sib), refs = refs[:7], refs[7:]
    mixed, token, found, source, lbuf, obuf, lsem, osem = refs[-8:]
    token[...] = jnp.zeros_like(token)
    slots, depth, outs = left.shape[0], lbuf.shape[0], obuf.shape[0]
    half = here.shape[1]
    bands = others.shape[0] + 1
    sector, band, core = where[phase], where[where.shape[0] - 2], where[where.shape[0] - 1]
    count = list_slots(own, sib, 0, sector, slots, found)

    def fetch(i, k):
        start_fetch(found[i], slots, left, left_sib, lbuf.at[k], lsem.at[k])

    def wait(k):
        pltpu.make_async_copy(left.at[0], lbuf.at[k], lsem.at[k]).wait()

    def out_copy(i, o):
        return pltpu.make_async_copy(obuf.at[o], mixed.at[found[i]], osem.at[o])

    def work(items, spots):
        for i, k in zip(items, spots):
            o = lax.rem(i, outs)

            @pl.when(i >= outs)
            def _():
                out_copy(i - outs, o).wait()

            obuf[o] = jnp.dot(lbuf[k], source[...], preferred_element_type=F32).astype(BF16)
            out_copy(i, o).start()

    for j in range(bands):
        b = lax.rem(band + j, bands)
        for i in range(CORES):
            c = core if i == 0 else 1 - core
            row = pl.multiple_of((b * CORES + c) * half, half)
            source[pl.ds(row, half)] = here[i] if j == 0 else others[j - 1, i]
    in_pairs(count, depth, fetch, wait, work)
    for back in range(outs, 0, -1):
        @pl.when(count >= back)
        def _():
            out_copy(count - back, lax.rem(count - back, outs)).wait()


def right_kernel(phase, *refs):
    own, sib, where, mixed, right, right_sib, keep, send, found, acc, mbuf, rbuf, msem, rsem = refs
    slots, depth = right.shape[0], rbuf.shape[0]
    half = keep.shape[1]
    bands = send.shape[0] + 1
    sector, band, core = where[phase], where[where.shape[0] - 2], where[where.shape[0] - 1]
    count = list_slots(own, sib, 1, sector, slots, found)

    def fetch(i, k):
        pltpu.make_async_copy(mixed.at[found[i]], mbuf.at[k], msem.at[k]).start()
        start_fetch(found[i], slots, right, right_sib, rbuf.at[k], rsem.at[k])

    def wait(k):
        pltpu.make_async_copy(mixed.at[0], mbuf.at[k], msem.at[k]).wait()
        pltpu.make_async_copy(right.at[0], rbuf.at[k], rsem.at[k]).wait()

    def work(items, spots):
        acc[...] += sum(
            lax.dot_general(mbuf[k], rbuf[k], (((1,), (1,)), ((), ())), preferred_element_type=F32) for k in spots
        )

    acc[...] = jnp.zeros_like(acc)
    in_pairs(count, depth, fetch, wait, work)
    for j in range(bands):
        b = lax.rem(band + j, bands)
        for i in range(CORES):
            c = core if i == 0 else 1 - core
            rows = acc[pl.ds(pl.multiple_of((b * CORES + c) * half, half), half)]
            if j == 0:
                keep[i] = rows
            else:
                send[j - 1, i] = rows.astype(BF16)


def local(devices, wavefunction, left, right, src, dst, live):
    slots, width = left.shape[0], left.shape[1]
    half = wavefunction.shape[0]
    sectors = half * devices // width
    bands = devices // (sectors * CORES)
    assert sectors == 4
    me = lax.axis_index("term")
    core, band, plane = me % CORES, (me // CORES) % bands, me // (CORES * bands)

    def move(value, to_plane=lambda a: a, band_step=0, flip=False):
        pairs = []
        for i in range(devices):
            c, b, a = i % CORES, (i // CORES) % bands, i // (CORES * bands)
            c = 1 - c if flip else c
            pairs.append((i, (to_plane(a) * bands + (b + band_step) % bands) * CORES + c))
        return lax.ppermute(value, "term", pairs)

    def beside(a):
        return a ^ 1

    def mirror(a):
        return 3 - a

    def bands_of(block):
        return jnp.stack([move(block, band_step=-j) for j in range(1, bands)])

    own_meta = jnp.concatenate([src, dst, live])
    sib_meta = move(own_meta, flip=True)
    mine = lax.dynamic_slice_in_dim(wavefunction, core * width, width, 1)
    theirs = lax.dynamic_slice_in_dim(wavefunction, (1 - core) * width, width, 1)
    from_sib = move(theirs, flip=True)
    left_sib, from_sib, sib_meta = lax.optimization_barrier((left, from_sib, sib_meta))
    left_sib = move(left_sib, flip=True)
    own_block = jnp.stack([mine, from_sib])
    mirror_block = move(own_block, mirror)
    beside_block, own_bands = lax.optimization_barrier((move(own_block, beside), bands_of(own_block)))
    far_block = move(mirror_block, beside)
    mirror_block, beside_bands, right_sib = lax.optimization_barrier((mirror_block, bands_of(beside_block), right))
    right_sib = move(right_sib, flip=True)
    mirror_bands = bands_of(mirror_block)
    blocks = [(own_block, own_bands), (beside_block, beside_bands), None, None]
    partner = plane ^ 1
    where_src = jnp.stack([plane, partner, 3 - plane, 3 - partner, band, core]).astype(jnp.int32)
    where_dst = jnp.stack([3 - partner, 3 - plane, partner, plane, band, core]).astype(jnp.int32)

    params = pltpu.CompilerParams(vmem_limit_bytes=VMEM)
    left_cost = pl.CostEstimate(flops=10**6, bytes_accessed=width, transcendentals=0)
    cost = pl.CostEstimate(flops=3 * 10**9, bytes_accessed=7 * width * width * 2, transcendentals=0)
    depth = 8
    mixed = None
    for phase in range(sectors):
        if phase == 1:
            far_block, mirror_bands, token = lax.optimization_barrier((far_block, mirror_bands, token))
            blocks[2:] = [(mirror_block, mirror_bands), (far_block, bands_of(far_block))]
        operands = [own_meta, sib_meta, where_src, *blocks[phase], left, left_sib]
        if mixed is not None:
            operands += [mixed, token]
        mixed, token = pl.pallas_call(
            functools.partial(left_kernel, phase),
            out_shape=(
                jax.ShapeDtypeStruct((CORES * slots, width, width), BF16),
                jax.ShapeDtypeStruct((8, 128), F32),
            ),
            in_specs=[SMEM] * 3 + [WHOLE] * 2 + [ANY] * (len(operands) - 5),
            out_specs=(ANY, WHOLE),
            scratch_shapes=[
                pltpu.SMEM((CORES * slots + 1,), jnp.int32),
                pltpu.VMEM((width, width), BF16),
                pltpu.VMEM((depth, width, width), BF16),
                pltpu.VMEM((4, width, width), BF16),
                pltpu.SemaphoreType.DMA((depth,)),
                pltpu.SemaphoreType.DMA((4,)),
            ],
            input_output_aliases={} if mixed is None else {7: 0},
            compiler_params=params,
            cost_estimate=left_cost,
            name="left_mix",
        )(*operands)

    def right_mix(phase, meta):
        keep, send = pl.pallas_call(
            functools.partial(right_kernel, phase),
            out_shape=(
                jax.ShapeDtypeStruct((CORES, half, width), F32),
                jax.ShapeDtypeStruct((bands - 1, CORES, half, width), BF16),
            ),
            in_specs=[SMEM] * 3 + [ANY] * 3,
            out_specs=(WHOLE, WHOLE),
            scratch_shapes=[
                pltpu.SMEM((CORES * slots + 1,), jnp.int32),
                pltpu.VMEM((width, width), F32),
                pltpu.VMEM((depth, width, width), BF16),
                pltpu.VMEM((depth, width, width), BF16),
                pltpu.SemaphoreType.DMA((depth,)),
                pltpu.SemaphoreType.DMA((depth,)),
            ],
            compiler_params=params,
            cost_estimate=cost,
            name="right_mix",
        )(meta, sib_meta, where_dst, mixed, right, right_sib)
        for j in range(1, bands):
            keep = keep + move(send[j - 1], band_step=j).astype(F32)
        return keep

    beside_far = right_mix(0, own_meta).astype(BF16)
    mirrored = right_mix(1, own_meta)
    meta, beside_far = lax.optimization_barrier((own_meta, beside_far))
    mirrored = (mirrored + move(beside_far, beside).astype(F32)).astype(BF16)
    beside_near = right_mix(2, meta).astype(BF16)
    total = right_mix(3, meta) + move(mirrored, mirror).astype(F32) + move(beside_near, beside).astype(F32)
    same, cross = total[0], move(total[1], flip=True)
    first = core == 0
    return jnp.concatenate([jnp.where(first, same, cross), jnp.where(first, cross, same)], axis=1)


def solution(mesh):
    spec = P(("parts", "term"))
    return jax.shard_map(
        functools.partial(local, mesh.shape["term"]),
        mesh=mesh,
        in_specs=(spec,) * 6,
        out_specs=spec,
        check_vma=False,
    )
```

```python
import functools

import jax
import jax.numpy as jnp
from jax import lax
from jax.experimental import pallas as pl
from jax.experimental.pallas import tpu as pltpu
from jax.sharding import PartitionSpec as P

F32, BF16 = jnp.float32, jnp.bfloat16
CORES = 2
VMEM = 16 * 1024 * 1024
ANY = pl.BlockSpec(memory_space=pl.ANY)
SMEM = pl.BlockSpec(memory_space=pltpu.SMEM)
WHOLE = pl.BlockSpec(memory_space=pltpu.VMEM)


def list_slots(own, sib, field, sector, slots, found):
    count = jnp.int32(0)
    for core, meta in enumerate((own, sib)):
        live = meta[2 * slots]
        for t in range(slots):
            found[count] = core * slots + t
            hit = jnp.logical_and(t < live, meta[field * slots + t] == sector)
            count = count + hit.astype(jnp.int32)
    return count


def in_pairs(count, depth, fetch, wait, work):
    for i in range(depth - 2):
        @pl.when(i < count)
        def _():
            fetch(i, i)

    def pair(p, carry):
        i = 2 * p
        for ahead in (i + depth - 2, i + depth - 1):
            @pl.when(ahead < count)
            def _():
                fetch(ahead, lax.rem(ahead, depth))
        spots = [lax.rem(i, depth), lax.rem(i, depth) + 1]
        for k in spots:
            wait(k)
        work((i, i + 1), spots)
        return carry

    lax.fori_loop(0, count // 2, pair, 0)

    @pl.when(count % 2 == 1)
    def _():
        k = lax.rem(count - 1, depth)
        wait(k)
        work((count - 1,), (k,))


def start_fetch(term, slots, own_hbm, sib_hbm, target, sem):
    @pl.when(term < slots)
    def _():
        pltpu.make_async_copy(own_hbm.at[term], target, sem).start()

    @pl.when(term >= slots)
    def _():
        pltpu.make_async_copy(sib_hbm.at[term - slots], target, sem).start()


def left_kernel(phase, *refs):
    (own, sib, where, here, others, left, left_sib), refs = refs[:7], refs[7:]
    mixed, found, source, lbuf, obuf, lsem, osem = refs[-7:]
    slots, depth, outs = left.shape[0], lbuf.shape[0], obuf.shape[0]
    half = here.shape[1]
    bands = others.shape[0] + 1
    sector, band, core = where[phase], where[where.shape[0] - 2], where[where.shape[0] - 1]
    count = list_slots(own, sib, 0, sector, slots, found)

    def fetch(i, k):
        start_fetch(found[i], slots, left, left_sib, lbuf.at[k], lsem.at[k])

    def wait(k):
        pltpu.make_async_copy(left.at[0], lbuf.at[k], lsem.at[k]).wait()

    def out_copy(i, o):
        return pltpu.make_async_copy(obuf.at[o], mixed.at[found[i]], osem.at[o])

    def work(items, spots):
        for i, k in zip(items, spots):
            o = lax.rem(i, outs)

            @pl.when(i >= outs)
            def _():
                out_copy(i - outs, o).wait()

            obuf[o] = jnp.dot(lbuf[k], source[...], preferred_element_type=F32).astype(BF16)
            out_copy(i, o).start()

    for j in range(bands):
        b = lax.rem(band + j, bands)
        for i in range(CORES):
            c = core if i == 0 else 1 - core
            row = pl.multiple_of((b * CORES + c) * half, half)
            source[pl.ds(row, half)] = here[i] if j == 0 else others[j - 1, i]
    in_pairs(count, depth, fetch, wait, work)
    for back in range(outs, 0, -1):
        @pl.when(count >= back)
        def _():
            out_copy(count - back, lax.rem(count - back, outs)).wait()


def right_kernel(phase, *refs):
    own, sib, where, mixed, right, right_sib, keep, send, found, acc, mbuf, rbuf, msem, rsem = refs
    slots, depth = right.shape[0], rbuf.shape[0]
    half = keep.shape[1]
    bands = send.shape[0] + 1
    sector, band, core = where[phase], where[where.shape[0] - 2], where[where.shape[0] - 1]
    count = list_slots(own, sib, 1, sector, slots, found)

    def fetch(i, k):
        pltpu.make_async_copy(mixed.at[found[i]], mbuf.at[k], msem.at[k]).start()
        start_fetch(found[i], slots, right, right_sib, rbuf.at[k], rsem.at[k])

    def wait(k):
        pltpu.make_async_copy(mixed.at[0], mbuf.at[k], msem.at[k]).wait()
        pltpu.make_async_copy(right.at[0], rbuf.at[k], rsem.at[k]).wait()

    def work(items, spots):
        acc[...] += sum(
            lax.dot_general(mbuf[k], rbuf[k], (((1,), (1,)), ((), ())), preferred_element_type=F32) for k in spots
        )

    acc[...] = jnp.zeros_like(acc)
    in_pairs(count, depth, fetch, wait, work)
    for j in range(bands):
        b = lax.rem(band + j, bands)
        for i in range(CORES):
            c = core if i == 0 else 1 - core
            rows = acc[pl.ds(pl.multiple_of((b * CORES + c) * half, half), half)]
            if j == 0:
                keep[i] = rows
            else:
                send[j - 1, i] = rows.astype(BF16)


def local(devices, wavefunction, left, right, src, dst, live):
    slots, width = left.shape[0], left.shape[1]
    half = wavefunction.shape[0]
    sectors = half * devices // width
    bands = devices // (sectors * CORES)
    assert sectors == 4
    me = lax.axis_index("term")
    core, band, plane = me % CORES, (me // CORES) % bands, me // (CORES * bands)

    def move(value, to_plane=lambda a: a, band_step=0, flip=False):
        pairs = []
        for i in range(devices):
            c, b, a = i % CORES, (i // CORES) % bands, i // (CORES * bands)
            c = 1 - c if flip else c
            pairs.append((i, (to_plane(a) * bands + (b + band_step) % bands) * CORES + c))
        return lax.ppermute(value, "term", pairs)

    def beside(a):
        return a ^ 1

    def mirror(a):
        return 3 - a

    def bands_of(block):
        return jnp.stack([move(block, band_step=-j) for j in range(1, bands)])

    own_meta = jnp.concatenate([src, dst, live])
    sib_meta = move(own_meta, flip=True)
    mine = lax.dynamic_slice_in_dim(wavefunction, core * width, width, 1)
    theirs = lax.dynamic_slice_in_dim(wavefunction, (1 - core) * width, width, 1)
    from_sib = move(theirs, flip=True)
    left_sib, from_sib, sib_meta = lax.optimization_barrier((left, from_sib, sib_meta))
    left_sib = move(left_sib, flip=True)
    own_block = jnp.stack([mine, from_sib])
    mirror_block = move(own_block, mirror)
    beside_block, own_bands = lax.optimization_barrier((move(own_block, beside), bands_of(own_block)))
    far_block = move(mirror_block, beside)
    mirror_block, beside_bands, right_sib = lax.optimization_barrier((mirror_block, bands_of(beside_block), right))
    right_sib = move(right_sib, flip=True)
    mirror_bands = bands_of(mirror_block)
    blocks = [(own_block, own_bands), (beside_block, beside_bands), None, None]
    partner = plane ^ 1
    where_src = jnp.stack([plane, partner, 3 - plane, 3 - partner, band, core]).astype(jnp.int32)
    where_dst = jnp.stack([3 - partner, 3 - plane, partner, plane, band, core]).astype(jnp.int32)

    params = pltpu.CompilerParams(vmem_limit_bytes=VMEM)
    cost = pl.CostEstimate(flops=3 * 10**9, bytes_accessed=7 * width * width * 2, transcendentals=0)
    depth = 8
    mixed = None
    for phase in range(sectors):
        if phase == 1:
            far_block, mirror_bands, mixed = lax.optimization_barrier((far_block, mirror_bands, mixed))
            blocks[2:] = [(mirror_block, mirror_bands), (far_block, bands_of(far_block))]
        operands = [own_meta, sib_meta, where_src, *blocks[phase], left, left_sib]
        if mixed is not None:
            operands.append(mixed)
        mixed = pl.pallas_call(
            functools.partial(left_kernel, phase),
            out_shape=jax.ShapeDtypeStruct((CORES * slots, width, width), BF16),
            in_specs=[SMEM] * 3 + [WHOLE] * 2 + [ANY] * (len(operands) - 5),
            out_specs=ANY,
            scratch_shapes=[
                pltpu.SMEM((CORES * slots + 1,), jnp.int32),
                pltpu.VMEM((width, width), BF16),
                pltpu.VMEM((depth, width, width), BF16),
                pltpu.VMEM((4, width, width), BF16),
                pltpu.SemaphoreType.DMA((depth,)),
                pltpu.SemaphoreType.DMA((4,)),
            ],
            input_output_aliases={} if mixed is None else {7: 0},
            compiler_params=params,
            cost_estimate=cost,
            name="left_mix",
        )(*operands)

    def right_mix(phase, meta):
        keep, send = pl.pallas_call(
            functools.partial(right_kernel, phase),
            out_shape=(
                jax.ShapeDtypeStruct((CORES, half, width), F32),
                jax.ShapeDtypeStruct((bands - 1, CORES, half, width), BF16),
            ),
            in_specs=[SMEM] * 3 + [ANY] * 3,
            out_specs=(WHOLE, WHOLE),
            scratch_shapes=[
                pltpu.SMEM((CORES * slots + 1,), jnp.int32),
                pltpu.VMEM((width, width), F32),
                pltpu.VMEM((depth, width, width), BF16),
                pltpu.VMEM((depth, width, width), BF16),
                pltpu.SemaphoreType.DMA((depth,)),
                pltpu.SemaphoreType.DMA((depth,)),
            ],
            compiler_params=params,
            cost_estimate=cost,
            name="right_mix",
        )(meta, sib_meta, where_dst, mixed, right, right_sib)
        for j in range(1, bands):
            keep = keep + move(send[j - 1], band_step=j).astype(F32)
        return keep

    beside_far = right_mix(0, own_meta).astype(BF16)
    mirrored = right_mix(1, own_meta)
    meta, beside_far = lax.optimization_barrier((own_meta, beside_far))
    mirrored = (mirrored + move(beside_far, beside).astype(F32)).astype(BF16)
    beside_near = right_mix(2, meta).astype(BF16)
    total = right_mix(3, meta) + move(mirrored, mirror).astype(F32) + move(beside_near, beside).astype(F32)
    same, cross = total[0], move(total[1], flip=True)
    first = core == 0
    return jnp.concatenate([jnp.where(first, same, cross), jnp.where(first, cross, same)], axis=1)


def solution(mesh):
    spec = P(("parts", "term"))
    return jax.shard_map(
        functools.partial(local, mesh.shape["term"]),
        mesh=mesh,
        in_specs=(spec,) * 6,
        out_specs=spec,
        check_vma=False,
    )
```

```python
import functools

import jax
import jax.numpy as jnp
from jax import lax
from jax.experimental import pallas as pl
from jax.experimental.pallas import tpu as pltpu
from jax.sharding import PartitionSpec as P

F32, BF16 = jnp.float32, jnp.bfloat16
CORES = 2
VMEM = 16 * 1024 * 1024
ANY = pl.BlockSpec(memory_space=pl.ANY)
SMEM = pl.BlockSpec(memory_space=pltpu.SMEM)
WHOLE = pl.BlockSpec(memory_space=pltpu.VMEM)


def list_slots(own, sib, field, sector, slots, found):
    count = jnp.int32(0)
    for core, meta in enumerate((own, sib)):
        live = meta[2 * slots]
        for t in range(slots):
            found[count] = core * slots + t
            hit = jnp.logical_and(t < live, meta[field * slots + t] == sector)
            count = count + hit.astype(jnp.int32)
    return count


def in_pairs(count, depth, fetch, wait, work):
    for i in range(depth - 2):
        @pl.when(i < count)
        def _():
            fetch(i, i)

    def pair(p, carry):
        i = 2 * p
        for ahead in (i + depth - 2, i + depth - 1):
            @pl.when(ahead < count)
            def _():
                fetch(ahead, lax.rem(ahead, depth))
        spots = [lax.rem(i, depth), lax.rem(i, depth) + 1]
        for k in spots:
            wait(k)
        work((i, i + 1), spots)
        return carry

    lax.fori_loop(0, count // 2, pair, 0)

    @pl.when(count % 2 == 1)
    def _():
        k = lax.rem(count - 1, depth)
        wait(k)
        work((count - 1,), (k,))


def start_fetch(term, slots, own_hbm, sib_hbm, target, sem):
    @pl.when(term < slots)
    def _():
        pltpu.make_async_copy(own_hbm.at[term], target, sem).start()

    @pl.when(term >= slots)
    def _():
        pltpu.make_async_copy(sib_hbm.at[term - slots], target, sem).start()


def left_kernel(phase, *refs):
    (own, sib, where, here, others, left, left_sib), refs = refs[:7], refs[7:]
    mixed, found, source, lbuf, obuf, lsem, osem = refs[-7:]
    slots, depth, outs = left.shape[0], lbuf.shape[0], obuf.shape[0]
    half = here.shape[1]
    bands = others.shape[0] + 1
    sector, band, core = where[phase], where[where.shape[0] - 2], where[where.shape[0] - 1]
    count = list_slots(own, sib, 0, sector, slots, found)

    def fetch(i, k):
        start_fetch(found[i], slots, left, left_sib, lbuf.at[k], lsem.at[k])

    def wait(k):
        pltpu.make_async_copy(left.at[0], lbuf.at[k], lsem.at[k]).wait()

    def out_copy(i, o):
        return pltpu.make_async_copy(obuf.at[o], mixed.at[found[i]], osem.at[o])

    def work(items, spots):
        for i, k in zip(items, spots):
            o = lax.rem(i, outs)

            @pl.when(i >= outs)
            def _():
                out_copy(i - outs, o).wait()

            obuf[o] = jnp.dot(lbuf[k], source[...], preferred_element_type=F32).astype(BF16)
            out_copy(i, o).start()

    for j in range(bands):
        b = lax.rem(band + j, bands)
        for i in range(CORES):
            c = core if i == 0 else 1 - core
            row = pl.multiple_of((b * CORES + c) * half, half)
            source[pl.ds(row, half)] = here[i] if j == 0 else others[j - 1, i]
    in_pairs(count, depth, fetch, wait, work)
    for back in range(outs, 0, -1):
        @pl.when(count >= back)
        def _():
            out_copy(count - back, lax.rem(count - back, outs)).wait()


def right_kernel(phase, *refs):
    own, sib, where, mixed, right, right_sib, keep, send, found, acc, mbuf, rbuf, msem, rsem = refs
    slots, depth = right.shape[0], rbuf.shape[0]
    half = keep.shape[1]
    bands = send.shape[0] + 1
    sector, band, core = where[phase], where[where.shape[0] - 2], where[where.shape[0] - 1]
    count = list_slots(own, sib, 1, sector, slots, found)

    def fetch(i, k):
        pltpu.make_async_copy(mixed.at[found[i]], mbuf.at[k], msem.at[k]).start()
        start_fetch(found[i], slots, right, right_sib, rbuf.at[k], rsem.at[k])

    def wait(k):
        pltpu.make_async_copy(mixed.at[0], mbuf.at[k], msem.at[k]).wait()
        pltpu.make_async_copy(right.at[0], rbuf.at[k], rsem.at[k]).wait()

    def work(items, spots):
        acc[...] += sum(
            lax.dot_general(mbuf[k], rbuf[k], (((1,), (1,)), ((), ())), preferred_element_type=F32) for k in spots
        )

    acc[...] = jnp.zeros_like(acc)
    in_pairs(count, depth, fetch, wait, work)
    for j in range(bands):
        b = lax.rem(band + j, bands)
        for i in range(CORES):
            c = core if i == 0 else 1 - core
            rows = acc[pl.ds(pl.multiple_of((b * CORES + c) * half, half), half)]
            if j == 0:
                keep[i] = rows
            else:
                send[j - 1, i] = rows.astype(BF16)


def local(devices, wavefunction, left, right, src, dst, live):
    slots, width = left.shape[0], left.shape[1]
    half = wavefunction.shape[0]
    sectors = half * devices // width
    bands = devices // (sectors * CORES)
    assert sectors == 4
    me = lax.axis_index("term")
    core, band, plane = me % CORES, (me // CORES) % bands, me // (CORES * bands)

    def move(value, to_plane=lambda a: a, band_step=0, flip=False):
        pairs = []
        for i in range(devices):
            c, b, a = i % CORES, (i // CORES) % bands, i // (CORES * bands)
            c = 1 - c if flip else c
            pairs.append((i, (to_plane(a) * bands + (b + band_step) % bands) * CORES + c))
        return lax.ppermute(value, "term", pairs)

    def beside(a):
        return a ^ 1

    def mirror(a):
        return 3 - a

    def bands_of(block):
        return jnp.stack([move(block, band_step=-j) for j in range(1, bands)])

    own_meta = jnp.concatenate([src, dst, live])
    sib_meta = move(own_meta, flip=True)
    mine = lax.dynamic_slice_in_dim(wavefunction, core * width, width, 1)
    theirs = lax.dynamic_slice_in_dim(wavefunction, (1 - core) * width, width, 1)
    from_sib = move(theirs, flip=True)
    left_sib, from_sib, sib_meta = lax.optimization_barrier((left, from_sib, sib_meta))
    left_sib = move(left_sib, flip=True)
    own_block = jnp.stack([mine, from_sib])
    beside_block, own_bands = lax.optimization_barrier((move(own_block, beside), bands_of(own_block)))
    beside_bands = bands_of(beside_block)
    mirror_block, beside_block, own_bands, right_sib = lax.optimization_barrier(
        (move(own_block, mirror), beside_block, own_bands, right)
    )
    right_sib = move(right_sib, flip=True)
    far_block = move(mirror_block, beside)
    mirror_bands = bands_of(mirror_block)
    blocks = [(own_block, own_bands), (beside_block, beside_bands), None, None]
    partner = plane ^ 1
    where_src = jnp.stack([plane, partner, 3 - plane, 3 - partner, band, core]).astype(jnp.int32)
    where_dst = jnp.stack([3 - partner, 3 - plane, partner, plane, band, core]).astype(jnp.int32)

    params = pltpu.CompilerParams(vmem_limit_bytes=VMEM)
    cost = pl.CostEstimate(flops=3 * 10**9, bytes_accessed=7 * width * width * 2, transcendentals=0)
    depth = 8
    mixed = None
    for phase in range(sectors):
        if phase == 1:
            far_block, mirror_bands, mixed = lax.optimization_barrier((far_block, mirror_bands, mixed))
            blocks[2:] = [(mirror_block, mirror_bands), (far_block, bands_of(far_block))]
        operands = [own_meta, sib_meta, where_src, *blocks[phase], left, left_sib]
        if mixed is not None:
            operands.append(mixed)
        mixed = pl.pallas_call(
            functools.partial(left_kernel, phase),
            out_shape=jax.ShapeDtypeStruct((CORES * slots, width, width), BF16),
            in_specs=[SMEM] * 3 + [WHOLE] * 2 + [ANY] * (len(operands) - 5),
            out_specs=ANY,
            scratch_shapes=[
                pltpu.SMEM((CORES * slots + 1,), jnp.int32),
                pltpu.VMEM((width, width), BF16),
                pltpu.VMEM((depth, width, width), BF16),
                pltpu.VMEM((4, width, width), BF16),
                pltpu.SemaphoreType.DMA((depth,)),
                pltpu.SemaphoreType.DMA((4,)),
            ],
            input_output_aliases={} if mixed is None else {7: 0},
            compiler_params=params,
            cost_estimate=cost,
            name="left_mix",
        )(*operands)

    def right_mix(phase):
        return pl.pallas_call(
            functools.partial(right_kernel, phase),
            out_shape=(
                jax.ShapeDtypeStruct((CORES, half, width), F32),
                jax.ShapeDtypeStruct((bands - 1, CORES, half, width), BF16),
            ),
            in_specs=[SMEM] * 3 + [ANY] * 3,
            out_specs=(WHOLE, WHOLE),
            scratch_shapes=[
                pltpu.SMEM((CORES * slots + 1,), jnp.int32),
                pltpu.VMEM((width, width), F32),
                pltpu.VMEM((depth, width, width), BF16),
                pltpu.VMEM((depth, width, width), BF16),
                pltpu.SemaphoreType.DMA((depth,)),
                pltpu.SemaphoreType.DMA((depth,)),
            ],
            compiler_params=params,
            cost_estimate=cost,
            name="right_mix",
        )(own_meta, sib_meta, where_dst, mixed, right, right_sib)

    def over_bands(keep, send):
        for j in range(1, bands):
            keep = keep + move(send[j - 1], band_step=j).astype(F32)
        return keep

    beside_far = over_bands(*right_mix(0)).astype(BF16)
    keep, send = right_mix(1)
    send, beside_far = lax.optimization_barrier((send, beside_far))
    mirrored = (over_bands(keep, send) + move(beside_far, beside).astype(F32)).astype(BF16)
    keep, send = right_mix(2)
    last_keep, last_send = right_mix(3)
    send, last_send, mirrored = lax.optimization_barrier((send, last_send, mirrored))
    beside_near = over_bands(keep, send).astype(BF16)
    last_send, beside_near = lax.optimization_barrier((last_send, beside_near))
    total = over_bands(last_keep, last_send) + move(mirrored, mirror).astype(F32) + move(beside_near, beside).astype(F32)
    same, cross = total[0], move(total[1], flip=True)
    first = core == 0
    return jnp.concatenate([jnp.where(first, same, cross), jnp.where(first, cross, same)], axis=1)


def solution(mesh):
    spec = P(("parts", "term"))
    return jax.shard_map(
        functools.partial(local, mesh.shape["term"]),
        mesh=mesh,
        in_specs=(spec,) * 6,
        out_specs=spec,
        check_vma=False,
    )
```

```python
import functools

import jax
import jax.numpy as jnp
from jax import lax
from jax.experimental import pallas as pl
from jax.experimental.pallas import tpu as pltpu
from jax.sharding import PartitionSpec as P

F32, BF16 = jnp.float32, jnp.bfloat16
CORES = 2
VMEM = 16 * 1024 * 1024
ANY = pl.BlockSpec(memory_space=pl.ANY)
SMEM = pl.BlockSpec(memory_space=pltpu.SMEM)
WHOLE = pl.BlockSpec(memory_space=pltpu.VMEM)


def list_slots(own, sib, field, sector, slots, found):
    count = jnp.int32(0)
    for core, meta in enumerate((own, sib)):
        live = meta[2 * slots]
        for t in range(slots):
            found[count] = core * slots + t
            hit = jnp.logical_and(t < live, meta[field * slots + t] == sector)
            count = count + hit.astype(jnp.int32)
    return count


def in_pairs(count, depth, fetch, wait, work):
    for i in range(depth - 2):
        @pl.when(i < count)
        def _():
            fetch(i, i)

    def pair(p, carry):
        i = 2 * p
        for ahead in (i + depth - 2, i + depth - 1):
            @pl.when(ahead < count)
            def _():
                fetch(ahead, lax.rem(ahead, depth))
        spots = [lax.rem(i, depth), lax.rem(i, depth) + 1]
        for k in spots:
            wait(k)
        work((i, i + 1), spots)
        return carry

    lax.fori_loop(0, count // 2, pair, 0)

    @pl.when(count % 2 == 1)
    def _():
        k = lax.rem(count - 1, depth)
        wait(k)
        work((count - 1,), (k,))


def start_fetch(term, slots, own_hbm, sib_hbm, target, sem):
    @pl.when(term < slots)
    def _():
        pltpu.make_async_copy(own_hbm.at[term], target, sem).start()

    @pl.when(term >= slots)
    def _():
        pltpu.make_async_copy(sib_hbm.at[term - slots], target, sem).start()


def left_kernel(phase, *refs):
    (own, sib, where, here, others, left, left_sib), refs = refs[:7], refs[7:]
    mixed, found, source, lbuf, obuf, lsem, osem = refs[-7:]
    slots, depth, outs = left.shape[0], lbuf.shape[0], obuf.shape[0]
    half = here.shape[1]
    bands = others.shape[0] + 1
    sector, band, core = where[phase], where[where.shape[0] - 2], where[where.shape[0] - 1]
    count = list_slots(own, sib, 0, sector, slots, found)

    def fetch(i, k):
        start_fetch(found[i], slots, left, left_sib, lbuf.at[k], lsem.at[k])

    def wait(k):
        pltpu.make_async_copy(left.at[0], lbuf.at[k], lsem.at[k]).wait()

    def out_copy(i, o):
        return pltpu.make_async_copy(obuf.at[o], mixed.at[found[i]], osem.at[o])

    def work(items, spots):
        for i, k in zip(items, spots):
            o = lax.rem(i, outs)

            @pl.when(i >= outs)
            def _():
                out_copy(i - outs, o).wait()

            obuf[o] = jnp.dot(lbuf[k], source[...], preferred_element_type=F32).astype(BF16)
            out_copy(i, o).start()

    for j in range(bands):
        b = lax.rem(band + j, bands)
        for i in range(CORES):
            c = core if i == 0 else 1 - core
            row = pl.multiple_of((b * CORES + c) * half, half)
            source[pl.ds(row, half)] = here[i] if j == 0 else others[j - 1, i]
    in_pairs(count, depth, fetch, wait, work)
    for back in range(outs, 0, -1):
        @pl.when(count >= back)
        def _():
            out_copy(count - back, lax.rem(count - back, outs)).wait()


def right_kernel(phase, *refs):
    own, sib, where, mixed, right, right_sib, keep, send, found, acc, mbuf, rbuf, msem, rsem = refs
    slots, depth = right.shape[0], rbuf.shape[0]
    half = keep.shape[1]
    bands = send.shape[0] + 1
    sector, band, core = where[phase], where[where.shape[0] - 2], where[where.shape[0] - 1]
    count = list_slots(own, sib, 1, sector, slots, found)

    def fetch(i, k):
        pltpu.make_async_copy(mixed.at[found[i]], mbuf.at[k], msem.at[k]).start()
        start_fetch(found[i], slots, right, right_sib, rbuf.at[k], rsem.at[k])

    def wait(k):
        pltpu.make_async_copy(mixed.at[0], mbuf.at[k], msem.at[k]).wait()
        pltpu.make_async_copy(right.at[0], rbuf.at[k], rsem.at[k]).wait()

    def work(items, spots):
        acc[...] += sum(
            lax.dot_general(mbuf[k], rbuf[k], (((1,), (1,)), ((), ())), preferred_element_type=F32) for k in spots
        )

    acc[...] = jnp.zeros_like(acc)
    in_pairs(count, depth, fetch, wait, work)
    for j in range(bands):
        b = lax.rem(band + j, bands)
        for i in range(CORES):
            c = core if i == 0 else 1 - core
            rows = acc[pl.ds(pl.multiple_of((b * CORES + c) * half, half), half)]
            if j == 0:
                keep[i] = rows
            else:
                send[j - 1, i] = rows.astype(BF16)


def local(devices, wavefunction, left, right, src, dst, live):
    slots, width = left.shape[0], left.shape[1]
    half = wavefunction.shape[0]
    sectors = half * devices // width
    bands = devices // (sectors * CORES)
    assert sectors == 4
    me = lax.axis_index("term")
    core, band, plane = me % CORES, (me // CORES) % bands, me // (CORES * bands)

    def move(value, to_plane=lambda a: a, band_step=0, flip=False):
        pairs = []
        for i in range(devices):
            c, b, a = i % CORES, (i // CORES) % bands, i // (CORES * bands)
            c = 1 - c if flip else c
            pairs.append((i, (to_plane(a) * bands + (b + band_step) % bands) * CORES + c))
        return lax.ppermute(value, "term", pairs)

    def beside(a):
        return a ^ 1

    def mirror(a):
        return 3 - a

    def bands_of(block):
        return jnp.stack([move(block, band_step=-j) for j in range(1, bands)])

    own_meta = jnp.concatenate([src, dst, live])
    sib_meta = move(own_meta, flip=True)
    mine = lax.dynamic_slice_in_dim(wavefunction, core * width, width, 1)
    theirs = lax.dynamic_slice_in_dim(wavefunction, (1 - core) * width, width, 1)
    from_sib = move(theirs, flip=True)
    left_sib, from_sib = lax.optimization_barrier((left, from_sib))
    left_sib = move(left_sib, flip=True)
    own_block = jnp.stack([mine, from_sib])
    mirror_block = move(own_block, mirror)
    beside_block, own_bands = lax.optimization_barrier((move(own_block, beside), bands_of(own_block)))
    far_block = move(mirror_block, beside)
    mirror_block, beside_bands, right_sib, sib_meta = lax.optimization_barrier(
        (mirror_block, bands_of(beside_block), right, sib_meta)
    )
    right_sib = move(right_sib, flip=True)
    mirror_bands = bands_of(mirror_block)
    blocks = [(own_block, own_bands), (beside_block, beside_bands), None, None]
    partner = plane ^ 1
    where_src = jnp.stack([plane, partner, 3 - plane, 3 - partner, band, core]).astype(jnp.int32)
    where_dst = jnp.stack([3 - partner, 3 - plane, partner, plane, band, core]).astype(jnp.int32)

    params = pltpu.CompilerParams(vmem_limit_bytes=VMEM)
    last_cost = pl.CostEstimate(flops=60 * 10**9, bytes_accessed=7 * width * width * 2, transcendentals=0)
    cost = pl.CostEstimate(flops=3 * 10**9, bytes_accessed=7 * width * width * 2, transcendentals=0)
    depth = 8
    mixed = None
    for phase in range(sectors):
        if phase == 1:
            far_block, mirror_bands, mixed = lax.optimization_barrier((far_block, mirror_bands, mixed))
            blocks[2:] = [(mirror_block, mirror_bands), (far_block, bands_of(far_block))]
        operands = [own_meta, sib_meta, where_src, *blocks[phase], left, left_sib]
        if mixed is not None:
            operands.append(mixed)
        mixed = pl.pallas_call(
            functools.partial(left_kernel, phase),
            out_shape=jax.ShapeDtypeStruct((CORES * slots, width, width), BF16),
            in_specs=[SMEM] * 3 + [WHOLE] * 2 + [ANY] * (len(operands) - 5),
            out_specs=ANY,
            scratch_shapes=[
                pltpu.SMEM((CORES * slots + 1,), jnp.int32),
                pltpu.VMEM((width, width), BF16),
                pltpu.VMEM((depth, width, width), BF16),
                pltpu.VMEM((4, width, width), BF16),
                pltpu.SemaphoreType.DMA((depth,)),
                pltpu.SemaphoreType.DMA((4,)),
            ],
            input_output_aliases={} if mixed is None else {7: 0},
            compiler_params=params,
            cost_estimate=last_cost if phase == sectors - 1 else cost,
            name="left_mix",
        )(*operands)

    def right_mix(phase, meta):
        keep, send = pl.pallas_call(
            functools.partial(right_kernel, phase),
            out_shape=(
                jax.ShapeDtypeStruct((CORES, half, width), F32),
                jax.ShapeDtypeStruct((bands - 1, CORES, half, width), BF16),
            ),
            in_specs=[SMEM] * 3 + [ANY] * 3,
            out_specs=(WHOLE, WHOLE),
            scratch_shapes=[
                pltpu.SMEM((CORES * slots + 1,), jnp.int32),
                pltpu.VMEM((width, width), F32),
                pltpu.VMEM((depth, width, width), BF16),
                pltpu.VMEM((depth, width, width), BF16),
                pltpu.SemaphoreType.DMA((depth,)),
                pltpu.SemaphoreType.DMA((depth,)),
            ],
            compiler_params=params,
            cost_estimate=cost,
            name="right_mix",
        )(meta, sib_meta, where_dst, mixed, right, right_sib)
        for j in range(1, bands):
            keep = keep + move(send[j - 1], band_step=j).astype(F32)
        return keep

    beside_far = right_mix(0, own_meta).astype(BF16)
    mirrored = right_mix(1, own_meta)
    meta, beside_far = lax.optimization_barrier((own_meta, beside_far))
    mirrored = (mirrored + move(beside_far, beside).astype(F32)).astype(BF16)
    beside_near = right_mix(2, meta).astype(BF16)
    total = right_mix(3, meta) + move(mirrored, mirror).astype(F32) + move(beside_near, beside).astype(F32)
    same, cross = total[0], move(total[1], flip=True)
    first = core == 0
    return jnp.concatenate([jnp.where(first, same, cross), jnp.where(first, cross, same)], axis=1)


def solution(mesh):
    spec = P(("parts", "term"))
    return jax.shard_map(
        functools.partial(local, mesh.shape["term"]),
        mesh=mesh,
        in_specs=(spec,) * 6,
        out_specs=spec,
        check_vma=False,
    )
```

```python
import functools

import jax
import jax.numpy as jnp
from jax import lax
from jax.experimental import pallas as pl
from jax.experimental.pallas import tpu as pltpu
from jax.sharding import PartitionSpec as P

F32, BF16 = jnp.float32, jnp.bfloat16
CORES = 2
VMEM = 16 * 1024 * 1024
ANY = pl.BlockSpec(memory_space=pl.ANY)
SMEM = pl.BlockSpec(memory_space=pltpu.SMEM)
WHOLE = pl.BlockSpec(memory_space=pltpu.VMEM)


def list_slots(own, sib, field, sector, slots, found):
    count = jnp.int32(0)
    for core, meta in enumerate((own, sib)):
        live = meta[2 * slots]
        for t in range(slots):
            found[count] = core * slots + t
            hit = jnp.logical_and(t < live, meta[field * slots + t] == sector)
            count = count + hit.astype(jnp.int32)
    return count


def in_pairs(count, depth, fetch, wait, work):
    for i in range(depth - 2):
        @pl.when(i < count)
        def _():
            fetch(i, i)

    def pair(p, carry):
        i = 2 * p
        for ahead in (i + depth - 2, i + depth - 1):
            @pl.when(ahead < count)
            def _():
                fetch(ahead, lax.rem(ahead, depth))
        spots = [lax.rem(i, depth), lax.rem(i, depth) + 1]
        for k in spots:
            wait(k)
        work((i, i + 1), spots)
        return carry

    lax.fori_loop(0, count // 2, pair, 0)

    @pl.when(count % 2 == 1)
    def _():
        k = lax.rem(count - 1, depth)
        wait(k)
        work((count - 1,), (k,))


def start_fetch(term, slots, own_hbm, sib_hbm, target, sem):
    @pl.when(term < slots)
    def _():
        pltpu.make_async_copy(own_hbm.at[term], target, sem).start()

    @pl.when(term >= slots)
    def _():
        pltpu.make_async_copy(sib_hbm.at[term - slots], target, sem).start()


def left_kernel(phase, *refs):
    (own, sib, where, here, others, left, left_sib), refs = refs[:7], refs[7:]
    mixed, found, source, lbuf, obuf, lsem, osem = refs[-7:]
    slots, depth, outs = left.shape[0], lbuf.shape[0], obuf.shape[0]
    half = here.shape[1]
    bands = others.shape[0] + 1
    sector, band, core = where[phase], where[where.shape[0] - 2], where[where.shape[0] - 1]
    count = list_slots(own, sib, 0, sector, slots, found)

    def fetch(i, k):
        start_fetch(found[i], slots, left, left_sib, lbuf.at[k], lsem.at[k])

    def wait(k):
        pltpu.make_async_copy(left.at[0], lbuf.at[k], lsem.at[k]).wait()

    def out_copy(i, o):
        return pltpu.make_async_copy(obuf.at[o], mixed.at[found[i]], osem.at[o])

    def work(items, spots):
        for i, k in zip(items, spots):
            o = lax.rem(i, outs)

            @pl.when(i >= outs)
            def _():
                out_copy(i - outs, o).wait()

            obuf[o] = jnp.dot(lbuf[k], source[...], preferred_element_type=F32).astype(BF16)
            out_copy(i, o).start()

    for j in range(bands):
        b = lax.rem(band + j, bands)
        for i in range(CORES):
            c = core if i == 0 else 1 - core
            row = pl.multiple_of((b * CORES + c) * half, half)
            source[pl.ds(row, half)] = here[i] if j == 0 else others[j - 1, i]
    in_pairs(count, depth, fetch, wait, work)
    for back in range(outs, 0, -1):
        @pl.when(count >= back)
        def _():
            out_copy(count - back, lax.rem(count - back, outs)).wait()


def right_kernel(phase, *refs):
    own, sib, where, mixed, right, right_sib, keep, send, found, acc, mbuf, rbuf, msem, rsem = refs
    slots, depth = right.shape[0], rbuf.shape[0]
    half = keep.shape[1]
    bands = send.shape[0] + 1
    sector, band, core = where[phase], where[where.shape[0] - 2], where[where.shape[0] - 1]
    count = list_slots(own, sib, 1, sector, slots, found)

    def fetch(i, k):
        pltpu.make_async_copy(mixed.at[found[i]], mbuf.at[k], msem.at[k]).start()
        start_fetch(found[i], slots, right, right_sib, rbuf.at[k], rsem.at[k])

    def wait(k):
        pltpu.make_async_copy(mixed.at[0], mbuf.at[k], msem.at[k]).wait()
        pltpu.make_async_copy(right.at[0], rbuf.at[k], rsem.at[k]).wait()

    def work(items, spots):
        acc[...] += sum(
            lax.dot_general(mbuf[k], rbuf[k], (((1,), (1,)), ((), ())), preferred_element_type=F32) for k in spots
        )

    acc[...] = jnp.zeros_like(acc)
    in_pairs(count, depth, fetch, wait, work)
    for j in range(bands):
        b = lax.rem(band + j, bands)
        for i in range(CORES):
            c = core if i == 0 else 1 - core
            rows = acc[pl.ds(pl.multiple_of((b * CORES + c) * half, half), half)]
            if j == 0:
                keep[i] = rows
            else:
                send[j - 1, i] = rows.astype(BF16)


def local(devices, wavefunction, left, right, src, dst, live):
    slots, width = left.shape[0], left.shape[1]
    half = wavefunction.shape[0]
    sectors = half * devices // width
    bands = devices // (sectors * CORES)
    assert sectors == 4
    me = lax.axis_index("term")
    core, band, plane = me % CORES, (me // CORES) % bands, me // (CORES * bands)

    def move(value, to_plane=lambda a: a, band_step=0, flip=False):
        pairs = []
        for i in range(devices):
            c, b, a = i % CORES, (i // CORES) % bands, i // (CORES * bands)
            c = 1 - c if flip else c
            pairs.append((i, (to_plane(a) * bands + (b + band_step) % bands) * CORES + c))
        return lax.ppermute(value, "term", pairs)

    def beside(a):
        return a ^ 1

    def mirror(a):
        return 3 - a

    def bands_of(block):
        return jnp.stack([move(block, band_step=-j) for j in range(1, bands)])

    own_meta = jnp.concatenate([src, dst, live])
    sib_meta = move(own_meta, flip=True)
    mine = lax.dynamic_slice_in_dim(wavefunction, core * width, width, 1)
    theirs = lax.dynamic_slice_in_dim(wavefunction, (1 - core) * width, width, 1)
    from_sib = move(theirs, flip=True)
    left_sib, from_sib = lax.optimization_barrier((left, from_sib))
    left_sib = move(left_sib, flip=True)
    own_block = jnp.stack([mine, from_sib])
    mirror_block = move(own_block, mirror)
    own_bands, beside_block = bands_of(own_block), move(own_block, beside)
    far_block = move(mirror_block, beside)
    mirror_block, own_bands, beside_bands, right_sib, sib_meta = lax.optimization_barrier(
        (mirror_block, own_bands, bands_of(beside_block), right, sib_meta)
    )
    right_sib = move(right_sib, flip=True)
    mirror_bands = bands_of(mirror_block)
    blocks = [(own_block, own_bands), (beside_block, beside_bands), None, None]
    partner = plane ^ 1
    where_src = jnp.stack([plane, partner, 3 - plane, 3 - partner, band, core]).astype(jnp.int32)
    where_dst = jnp.stack([3 - partner, 3 - plane, partner, plane, band, core]).astype(jnp.int32)

    params = pltpu.CompilerParams(vmem_limit_bytes=VMEM)
    last_cost = pl.CostEstimate(flops=60 * 10**9, bytes_accessed=7 * width * width * 2, transcendentals=0)
    cost = pl.CostEstimate(flops=3 * 10**9, bytes_accessed=7 * width * width * 2, transcendentals=0)
    depth = 8
    mixed = None
    for phase in range(sectors):
        if phase == 1:
            far_block, mirror_bands, mixed = lax.optimization_barrier((far_block, mirror_bands, mixed))
            blocks[2:] = [(mirror_block, mirror_bands), (far_block, bands_of(far_block))]
        operands = [own_meta, sib_meta, where_src, *blocks[phase], left, left_sib]
        if mixed is not None:
            operands.append(mixed)
        mixed = pl.pallas_call(
            functools.partial(left_kernel, phase),
            out_shape=jax.ShapeDtypeStruct((CORES * slots, width, width), BF16),
            in_specs=[SMEM] * 3 + [WHOLE] * 2 + [ANY] * (len(operands) - 5),
            out_specs=ANY,
            scratch_shapes=[
                pltpu.SMEM((CORES * slots + 1,), jnp.int32),
                pltpu.VMEM((width, width), BF16),
                pltpu.VMEM((depth, width, width), BF16),
                pltpu.VMEM((4, width, width), BF16),
                pltpu.SemaphoreType.DMA((depth,)),
                pltpu.SemaphoreType.DMA((4,)),
            ],
            input_output_aliases={} if mixed is None else {7: 0},
            compiler_params=params,
            cost_estimate=last_cost if phase == sectors - 1 else cost,
            name="left_mix",
        )(*operands)

    def right_mix(phase, meta):
        keep, send = pl.pallas_call(
            functools.partial(right_kernel, phase),
            out_shape=(
                jax.ShapeDtypeStruct((CORES, half, width), F32),
                jax.ShapeDtypeStruct((bands - 1, CORES, half, width), BF16),
            ),
            in_specs=[SMEM] * 3 + [ANY] * 3,
            out_specs=(WHOLE, WHOLE),
            scratch_shapes=[
                pltpu.SMEM((CORES * slots + 1,), jnp.int32),
                pltpu.VMEM((width, width), F32),
                pltpu.VMEM((depth, width, width), BF16),
                pltpu.VMEM((depth, width, width), BF16),
                pltpu.SemaphoreType.DMA((depth,)),
                pltpu.SemaphoreType.DMA((depth,)),
            ],
            compiler_params=params,
            cost_estimate=cost,
            name="right_mix",
        )(meta, sib_meta, where_dst, mixed, right, right_sib)
        for j in range(1, bands):
            keep = keep + move(send[j - 1], band_step=j).astype(F32)
        return keep

    beside_far = right_mix(0, own_meta).astype(BF16)
    mirrored = right_mix(1, own_meta)
    meta, beside_far = lax.optimization_barrier((own_meta, beside_far))
    mirrored = (mirrored + move(beside_far, beside).astype(F32)).astype(BF16)
    beside_near = right_mix(2, meta).astype(BF16)
    total = right_mix(3, meta) + move(mirrored, mirror).astype(F32) + move(beside_near, beside).astype(F32)
    same, cross = total[0], move(total[1], flip=True)
    first = core == 0
    return jnp.concatenate([jnp.where(first, same, cross), jnp.where(first, cross, same)], axis=1)


def solution(mesh):
    spec = P(("parts", "term"))
    return jax.shard_map(
        functools.partial(local, mesh.shape["term"]),
        mesh=mesh,
        in_specs=(spec,) * 6,
        out_specs=spec,
        check_vma=False,
    )
```

```python
import functools

import jax
import jax.numpy as jnp
from jax import lax
from jax.experimental import pallas as pl
from jax.experimental.pallas import tpu as pltpu
from jax.sharding import PartitionSpec as P

F32, BF16 = jnp.float32, jnp.bfloat16
CORES = 2
VMEM = 16 * 1024 * 1024
ANY = pl.BlockSpec(memory_space=pl.ANY)
SMEM = pl.BlockSpec(memory_space=pltpu.SMEM)
WHOLE = pl.BlockSpec(memory_space=pltpu.VMEM)


def list_slots(own, sib, field, sector, slots, found):
    count = jnp.int32(0)
    for core, meta in enumerate((own, sib)):
        live = meta[2 * slots]
        for t in range(slots):
            found[count] = core * slots + t
            hit = jnp.logical_and(t < live, meta[field * slots + t] == sector)
            count = count + hit.astype(jnp.int32)
    return count


def in_pairs(count, depth, fetch, wait, work):
    for i in range(depth - 2):
        @pl.when(i < count)
        def _():
            fetch(i, i)

    def pair(p, carry):
        i = 2 * p
        for ahead in (i + depth - 2, i + depth - 1):
            @pl.when(ahead < count)
            def _():
                fetch(ahead, lax.rem(ahead, depth))
        spots = [lax.rem(i, depth), lax.rem(i, depth) + 1]
        for k in spots:
            wait(k)
        work((i, i + 1), spots)
        return carry

    lax.fori_loop(0, count // 2, pair, 0)

    @pl.when(count % 2 == 1)
    def _():
        k = lax.rem(count - 1, depth)
        wait(k)
        work((count - 1,), (k,))


def start_fetch(term, slots, own_hbm, sib_hbm, target, sem):
    @pl.when(term < slots)
    def _():
        pltpu.make_async_copy(own_hbm.at[term], target, sem).start()

    @pl.when(term >= slots)
    def _():
        pltpu.make_async_copy(sib_hbm.at[term - slots], target, sem).start()


def left_kernel(phase, *refs):
    (own, sib, where, here, others, left, left_sib), refs = refs[:7], refs[7:]
    mixed, found, source, lbuf, obuf, lsem, osem = refs[-7:]
    slots, depth, outs = left.shape[0], lbuf.shape[0], obuf.shape[0]
    half = here.shape[1]
    bands = others.shape[0] + 1
    sector, band, core = where[phase], where[where.shape[0] - 2], where[where.shape[0] - 1]
    count = list_slots(own, sib, 0, sector, slots, found)

    def fetch(i, k):
        start_fetch(found[i], slots, left, left_sib, lbuf.at[k], lsem.at[k])

    def wait(k):
        pltpu.make_async_copy(left.at[0], lbuf.at[k], lsem.at[k]).wait()

    def out_copy(i, o):
        return pltpu.make_async_copy(obuf.at[o], mixed.at[found[i]], osem.at[o])

    def work(items, spots):
        for i, k in zip(items, spots):
            o = lax.rem(i, outs)

            @pl.when(i >= outs)
            def _():
                out_copy(i - outs, o).wait()

            obuf[o] = jnp.dot(lbuf[k], source[...], preferred_element_type=F32).astype(BF16)
            out_copy(i, o).start()

    for j in range(bands):
        b = lax.rem(band + j, bands)
        for i in range(CORES):
            c = core if i == 0 else 1 - core
            row = pl.multiple_of((b * CORES + c) * half, half)
            source[pl.ds(row, half)] = here[i] if j == 0 else others[j - 1, i]
    in_pairs(count, depth, fetch, wait, work)
    for back in range(outs, 0, -1):
        @pl.when(count >= back)
        def _():
            out_copy(count - back, lax.rem(count - back, outs)).wait()


def right_kernel(phase, *refs):
    own, sib, where, mixed, right, right_sib, keep, send, found, acc, mbuf, rbuf, msem, rsem = refs
    slots, depth = right.shape[0], rbuf.shape[0]
    half = keep.shape[1]
    bands = send.shape[0] + 1
    sector, band, core = where[phase], where[where.shape[0] - 2], where[where.shape[0] - 1]
    count = list_slots(own, sib, 1, sector, slots, found)

    def fetch(i, k):
        pltpu.make_async_copy(mixed.at[found[i]], mbuf.at[k], msem.at[k]).start()
        start_fetch(found[i], slots, right, right_sib, rbuf.at[k], rsem.at[k])

    def wait(k):
        pltpu.make_async_copy(mixed.at[0], mbuf.at[k], msem.at[k]).wait()
        pltpu.make_async_copy(right.at[0], rbuf.at[k], rsem.at[k]).wait()

    def work(items, spots):
        acc[...] += sum(
            lax.dot_general(mbuf[k], rbuf[k], (((1,), (1,)), ((), ())), preferred_element_type=F32) for k in spots
        )

    acc[...] = jnp.zeros_like(acc)
    in_pairs(count, depth, fetch, wait, work)
    for j in range(bands):
        b = lax.rem(band + j, bands)
        for i in range(CORES):
            c = core if i == 0 else 1 - core
            rows = acc[pl.ds(pl.multiple_of((b * CORES + c) * half, half), half)]
            if j == 0:
                keep[i] = rows
            else:
                send[j - 1, i] = rows.astype(BF16)


def local(devices, wavefunction, left, right, src, dst, live):
    slots, width = left.shape[0], left.shape[1]
    half = wavefunction.shape[0]
    sectors = half * devices // width
    bands = devices // (sectors * CORES)
    assert sectors == 4
    me = lax.axis_index("term")
    core, band, plane = me % CORES, (me // CORES) % bands, me // (CORES * bands)

    def move(value, to_plane=lambda a: a, band_step=0, flip=False):
        pairs = []
        for i in range(devices):
            c, b, a = i % CORES, (i // CORES) % bands, i // (CORES * bands)
            c = 1 - c if flip else c
            pairs.append((i, (to_plane(a) * bands + (b + band_step) % bands) * CORES + c))
        return lax.ppermute(value, "term", pairs)

    def beside(a):
        return a ^ 1

    def mirror(a):
        return 3 - a

    def bands_of(block):
        return jnp.stack([move(block, band_step=-j) for j in range(1, bands)])

    own_meta = jnp.concatenate([src, dst, live])
    sib_meta = move(own_meta, flip=True)
    mine = lax.dynamic_slice_in_dim(wavefunction, core * width, width, 1)
    theirs = lax.dynamic_slice_in_dim(wavefunction, (1 - core) * width, width, 1)
    from_sib = move(theirs, flip=True)
    left_sib, from_sib = lax.optimization_barrier((left, from_sib))
    left_sib = move(left_sib, flip=True)
    own_block = jnp.stack([mine, from_sib])
    mirror_block = move(own_block, mirror)
    own_bands, beside_block = bands_of(own_block), move(own_block, beside)
    beside_bands = bands_of(beside_block)
    blocks = [(own_block, own_bands), None, None, None]
    partner = plane ^ 1
    where_src = jnp.stack([plane, partner, 3 - plane, 3 - partner, band, core]).astype(jnp.int32)
    where_dst = jnp.stack([3 - partner, 3 - plane, partner, plane, band, core]).astype(jnp.int32)

    params = pltpu.CompilerParams(vmem_limit_bytes=VMEM)
    last_cost = pl.CostEstimate(flops=60 * 10**9, bytes_accessed=7 * width * width * 2, transcendentals=0)
    cost = pl.CostEstimate(flops=3 * 10**9, bytes_accessed=7 * width * width * 2, transcendentals=0)
    depth = 8
    mixed = None
    for phase in range(sectors):
        if phase == 1:
            mirror_block, mixed = lax.optimization_barrier((mirror_block, mixed))
            far_block = move(mirror_block, beside)
            mirror_block, beside_bands, right_sib = lax.optimization_barrier((mirror_block, beside_bands, right))
            right_sib = move(right_sib, flip=True)
            far_block, mirror_bands = lax.optimization_barrier((far_block, bands_of(mirror_block)))
            far_bands = bands_of(far_block)
            blocks[1:] = [(beside_block, beside_bands), (mirror_block, mirror_bands), (far_block, far_bands)]
        operands = [own_meta, sib_meta, where_src, *blocks[phase], left, left_sib]
        if mixed is not None:
            operands.append(mixed)
        mixed = pl.pallas_call(
            functools.partial(left_kernel, phase),
            out_shape=jax.ShapeDtypeStruct((CORES * slots, width, width), BF16),
            in_specs=[SMEM] * 3 + [WHOLE] * 2 + [ANY] * (len(operands) - 5),
            out_specs=ANY,
            scratch_shapes=[
                pltpu.SMEM((CORES * slots + 1,), jnp.int32),
                pltpu.VMEM((width, width), BF16),
                pltpu.VMEM((depth, width, width), BF16),
                pltpu.VMEM((4, width, width), BF16),
                pltpu.SemaphoreType.DMA((depth,)),
                pltpu.SemaphoreType.DMA((4,)),
            ],
            input_output_aliases={} if mixed is None else {7: 0},
            compiler_params=params,
            cost_estimate=last_cost if phase == sectors - 1 else cost,
            name="left_mix",
        )(*operands)

    def right_mix(phase, meta):
        keep, send = pl.pallas_call(
            functools.partial(right_kernel, phase),
            out_shape=(
                jax.ShapeDtypeStruct((CORES, half, width), F32),
                jax.ShapeDtypeStruct((bands - 1, CORES, half, width), BF16),
            ),
            in_specs=[SMEM] * 3 + [ANY] * 3,
            out_specs=(WHOLE, WHOLE),
            scratch_shapes=[
                pltpu.SMEM((CORES * slots + 1,), jnp.int32),
                pltpu.VMEM((width, width), F32),
                pltpu.VMEM((depth, width, width), BF16),
                pltpu.VMEM((depth, width, width), BF16),
                pltpu.SemaphoreType.DMA((depth,)),
                pltpu.SemaphoreType.DMA((depth,)),
            ],
            compiler_params=params,
            cost_estimate=cost,
            name="right_mix",
        )(meta, sib_meta, where_dst, mixed, right, right_sib)
        for j in range(1, bands):
            keep = keep + move(send[j - 1], band_step=j).astype(F32)
        return keep

    beside_far = right_mix(0, own_meta).astype(BF16)
    mirrored = right_mix(1, own_meta)
    meta, beside_far = lax.optimization_barrier((own_meta, beside_far))
    mirrored = (mirrored + move(beside_far, beside).astype(F32)).astype(BF16)
    beside_near = right_mix(2, meta).astype(BF16)
    total = right_mix(3, meta) + move(mirrored, mirror).astype(F32) + move(beside_near, beside).astype(F32)
    same, cross = total[0], move(total[1], flip=True)
    first = core == 0
    return jnp.concatenate([jnp.where(first, same, cross), jnp.where(first, cross, same)], axis=1)


def solution(mesh):
    spec = P(("parts", "term"))
    return jax.shard_map(
        functools.partial(local, mesh.shape["term"]),
        mesh=mesh,
        in_specs=(spec,) * 6,
        out_specs=spec,
        check_vma=False,
    )
```

```python
import functools

import jax
import jax.numpy as jnp
from jax import lax
from jax.experimental import pallas as pl
from jax.experimental.pallas import tpu as pltpu
from jax.sharding import PartitionSpec as P

F32, BF16 = jnp.float32, jnp.bfloat16
CORES = 2
VMEM = 16 * 1024 * 1024
ANY = pl.BlockSpec(memory_space=pl.ANY)
SMEM = pl.BlockSpec(memory_space=pltpu.SMEM)
WHOLE = pl.BlockSpec(memory_space=pltpu.VMEM)


def list_slots(own, sib, field, sector, slots, found):
    count = jnp.int32(0)
    for core, meta in enumerate((own, sib)):
        live = meta[2 * slots]
        for t in range(slots):
            found[count] = core * slots + t
            hit = jnp.logical_and(t < live, meta[field * slots + t] == sector)
            count = count + hit.astype(jnp.int32)
    return count


def in_pairs(count, depth, fetch, wait, work):
    for i in range(depth - 2):
        @pl.when(i < count)
        def _():
            fetch(i, i)

    def pair(p, carry):
        i = 2 * p
        for ahead in (i + depth - 2, i + depth - 1):
            @pl.when(ahead < count)
            def _():
                fetch(ahead, lax.rem(ahead, depth))
        spots = [lax.rem(i, depth), lax.rem(i, depth) + 1]
        for k in spots:
            wait(k)
        work((i, i + 1), spots)
        return carry

    lax.fori_loop(0, count // 2, pair, 0)

    @pl.when(count % 2 == 1)
    def _():
        k = lax.rem(count - 1, depth)
        wait(k)
        work((count - 1,), (k,))


def start_fetch(term, slots, own_hbm, sib_hbm, target, sem):
    @pl.when(term < slots)
    def _():
        pltpu.make_async_copy(own_hbm.at[term], target, sem).start()

    @pl.when(term >= slots)
    def _():
        pltpu.make_async_copy(sib_hbm.at[term - slots], target, sem).start()


def left_kernel(phase, *refs):
    (own, sib, where, here, others, left, left_sib), refs = refs[:7], refs[7:]
    mixed, found, source, lbuf, obuf, lsem, osem = refs[-7:]
    slots, depth, outs = left.shape[0], lbuf.shape[0], obuf.shape[0]
    half = here.shape[1]
    bands = others.shape[0] + 1
    sector, band, core = where[phase], where[where.shape[0] - 2], where[where.shape[0] - 1]
    count = list_slots(own, sib, 0, sector, slots, found)

    def fetch(i, k):
        start_fetch(found[i], slots, left, left_sib, lbuf.at[k], lsem.at[k])

    def wait(k):
        pltpu.make_async_copy(left.at[0], lbuf.at[k], lsem.at[k]).wait()

    def out_copy(i, o):
        return pltpu.make_async_copy(obuf.at[o], mixed.at[found[i]], osem.at[o])

    def work(items, spots):
        for i, k in zip(items, spots):
            o = lax.rem(i, outs)

            @pl.when(i >= outs)
            def _():
                out_copy(i - outs, o).wait()

            obuf[o] = jnp.dot(lbuf[k], source[...], preferred_element_type=F32).astype(BF16)
            out_copy(i, o).start()

    for j in range(bands):
        b = lax.rem(band + j, bands)
        for i in range(CORES):
            c = core if i == 0 else 1 - core
            row = pl.multiple_of((b * CORES + c) * half, half)
            source[pl.ds(row, half)] = here[i] if j == 0 else others[j - 1, i]
    in_pairs(count, depth, fetch, wait, work)
    for back in range(outs, 0, -1):
        @pl.when(count >= back)
        def _():
            out_copy(count - back, lax.rem(count - back, outs)).wait()


def right_kernel(phase, *refs):
    own, sib, where, mixed, right, right_sib, keep, send, found, acc, mbuf, rbuf, msem, rsem = refs
    slots, depth = right.shape[0], rbuf.shape[0]
    half = keep.shape[1]
    bands = send.shape[0] + 1
    sector, band, core = where[phase], where[where.shape[0] - 2], where[where.shape[0] - 1]
    count = list_slots(own, sib, 1, sector, slots, found)

    def fetch(i, k):
        pltpu.make_async_copy(mixed.at[found[i]], mbuf.at[k], msem.at[k]).start()
        start_fetch(found[i], slots, right, right_sib, rbuf.at[k], rsem.at[k])

    def wait(k):
        pltpu.make_async_copy(mixed.at[0], mbuf.at[k], msem.at[k]).wait()
        pltpu.make_async_copy(right.at[0], rbuf.at[k], rsem.at[k]).wait()

    def work(items, spots):
        acc[...] += sum(
            lax.dot_general(mbuf[k], rbuf[k], (((1,), (1,)), ((), ())), preferred_element_type=F32) for k in spots
        )

    acc[...] = jnp.zeros_like(acc)
    in_pairs(count, depth, fetch, wait, work)
    for j in range(bands):
        b = lax.rem(band + j, bands)
        for i in range(CORES):
            c = core if i == 0 else 1 - core
            rows = acc[pl.ds(pl.multiple_of((b * CORES + c) * half, half), half)]
            if j == 0:
                keep[i] = rows
            else:
                send[j - 1, i] = rows.astype(BF16)


def local(devices, wavefunction, left, right, src, dst, live):
    slots, width = left.shape[0], left.shape[1]
    half = wavefunction.shape[0]
    sectors = half * devices // width
    bands = devices // (sectors * CORES)
    assert sectors == 4
    me = lax.axis_index("term")
    core, band, plane = me % CORES, (me // CORES) % bands, me // (CORES * bands)

    def move(value, to_plane=lambda a: a, band_step=0, flip=False):
        pairs = []
        for i in range(devices):
            c, b, a = i % CORES, (i // CORES) % bands, i // (CORES * bands)
            c = 1 - c if flip else c
            pairs.append((i, (to_plane(a) * bands + (b + band_step) % bands) * CORES + c))
        return lax.ppermute(value, "term", pairs)

    def beside(a):
        return a ^ 1

    def mirror(a):
        return 3 - a

    def bands_of(block):
        return jnp.stack([move(block, band_step=-j) for j in range(1, bands)])

    own_meta = jnp.concatenate([src, dst, live])
    mine = lax.dynamic_slice_in_dim(wavefunction, core * width, width, 1)
    theirs = lax.dynamic_slice_in_dim(wavefunction, (1 - core) * width, width, 1)
    from_sib = move(theirs, flip=True)
    left_sib, from_sib, own_meta = lax.optimization_barrier((left, from_sib, own_meta))
    sib_meta = move(own_meta, flip=True)
    left_sib = move(left_sib, flip=True)
    own_block = jnp.stack([mine, from_sib])
    mirror_block = move(own_block, mirror)
    own_bands, beside_block = bands_of(own_block), move(own_block, beside)
    beside_bands = bands_of(beside_block)
    blocks = [(own_block, own_bands), None, None, None]
    partner = plane ^ 1
    where_src = jnp.stack([plane, partner, 3 - plane, 3 - partner, band, core]).astype(jnp.int32)
    where_dst = jnp.stack([3 - partner, 3 - plane, partner, plane, band, core]).astype(jnp.int32)

    params = pltpu.CompilerParams(vmem_limit_bytes=VMEM)
    last_cost = pl.CostEstimate(flops=60 * 10**9, bytes_accessed=7 * width * width * 2, transcendentals=0)
    cost = pl.CostEstimate(flops=3 * 10**9, bytes_accessed=7 * width * width * 2, transcendentals=0)
    depth = 8
    mixed = None
    for phase in range(sectors):
        if phase == 1:
            mirror_block, mixed = lax.optimization_barrier((mirror_block, mixed))
            far_block = move(mirror_block, beside)
            mirror_block, beside_bands, right_sib = lax.optimization_barrier((mirror_block, beside_bands, right))
            right_sib = move(right_sib, flip=True)
            far_block, mirror_bands = lax.optimization_barrier((far_block, bands_of(mirror_block)))
            far_bands = bands_of(far_block)
            blocks[1:] = [(beside_block, beside_bands), (mirror_block, mirror_bands), (far_block, far_bands)]
        operands = [own_meta, sib_meta, where_src, *blocks[phase], left, left_sib]
        if mixed is not None:
            operands.append(mixed)
        mixed = pl.pallas_call(
            functools.partial(left_kernel, phase),
            out_shape=jax.ShapeDtypeStruct((CORES * slots, width, width), BF16),
            in_specs=[SMEM] * 3 + [WHOLE] * 2 + [ANY] * (len(operands) - 5),
            out_specs=ANY,
            scratch_shapes=[
                pltpu.SMEM((CORES * slots + 1,), jnp.int32),
                pltpu.VMEM((width, width), BF16),
                pltpu.VMEM((depth, width, width), BF16),
                pltpu.VMEM((4, width, width), BF16),
                pltpu.SemaphoreType.DMA((depth,)),
                pltpu.SemaphoreType.DMA((4,)),
            ],
            input_output_aliases={} if mixed is None else {7: 0},
            compiler_params=params,
            cost_estimate=last_cost if phase == sectors - 1 else cost,
            name="left_mix",
        )(*operands)

    def right_mix(phase, meta):
        keep, send = pl.pallas_call(
            functools.partial(right_kernel, phase),
            out_shape=(
                jax.ShapeDtypeStruct((CORES, half, width), F32),
                jax.ShapeDtypeStruct((bands - 1, CORES, half, width), BF16),
            ),
            in_specs=[SMEM] * 3 + [ANY] * 3,
            out_specs=(WHOLE, WHOLE),
            scratch_shapes=[
                pltpu.SMEM((CORES * slots + 1,), jnp.int32),
                pltpu.VMEM((width, width), F32),
                pltpu.VMEM((depth, width, width), BF16),
                pltpu.VMEM((depth, width, width), BF16),
                pltpu.SemaphoreType.DMA((depth,)),
                pltpu.SemaphoreType.DMA((depth,)),
            ],
            compiler_params=params,
            cost_estimate=cost,
            name="right_mix",
        )(meta, sib_meta, where_dst, mixed, right, right_sib)
        for j in range(1, bands):
            keep = keep + move(send[j - 1], band_step=j).astype(F32)
        return keep

    beside_far = right_mix(0, own_meta).astype(BF16)
    mirrored = right_mix(1, own_meta)
    meta, beside_far = lax.optimization_barrier((own_meta, beside_far))
    mirrored = (mirrored + move(beside_far, beside).astype(F32)).astype(BF16)
    beside_near = right_mix(2, meta).astype(BF16)
    total = right_mix(3, meta) + move(mirrored, mirror).astype(F32) + move(beside_near, beside).astype(F32)
    same, cross = total[0], move(total[1], flip=True)
    first = core == 0
    return jnp.concatenate([jnp.where(first, same, cross), jnp.where(first, cross, same)], axis=1)


def solution(mesh):
    spec = P(("parts", "term"))
    return jax.shard_map(
        functools.partial(local, mesh.shape["term"]),
        mesh=mesh,
        in_specs=(spec,) * 6,
        out_specs=spec,
        check_vma=False,
    )
```

```python
import functools

import jax
import jax.numpy as jnp
from jax import lax
from jax.experimental import pallas as pl
from jax.experimental.pallas import tpu as pltpu
from jax.sharding import PartitionSpec as P

F32, BF16 = jnp.float32, jnp.bfloat16
CORES = 2
VMEM = 16 * 1024 * 1024
ANY = pl.BlockSpec(memory_space=pl.ANY)
SMEM = pl.BlockSpec(memory_space=pltpu.SMEM)
WHOLE = pl.BlockSpec(memory_space=pltpu.VMEM)


def list_slots(own, sib, field, sector, slots, found):
    count = jnp.int32(0)
    for core, meta in enumerate((own, sib)):
        live = meta[2 * slots]
        for t in range(slots):
            found[count] = core * slots + t
            hit = jnp.logical_and(t < live, meta[field * slots + t] == sector)
            count = count + hit.astype(jnp.int32)
    return count


def in_pairs(count, depth, fetch, wait, work):
    for i in range(depth - 2):
        @pl.when(i < count)
        def _():
            fetch(i, i)

    def pair(p, carry):
        i = 2 * p
        for ahead in (i + depth - 2, i + depth - 1):
            @pl.when(ahead < count)
            def _():
                fetch(ahead, lax.rem(ahead, depth))
        spots = [lax.rem(i, depth), lax.rem(i, depth) + 1]
        for k in spots:
            wait(k)
        work((i, i + 1), spots)
        return carry

    lax.fori_loop(0, count // 2, pair, 0)

    @pl.when(count % 2 == 1)
    def _():
        k = lax.rem(count - 1, depth)
        wait(k)
        work((count - 1,), (k,))


def start_fetch(term, slots, own_hbm, sib_hbm, target, sem):
    @pl.when(term < slots)
    def _():
        pltpu.make_async_copy(own_hbm.at[term], target, sem).start()

    @pl.when(term >= slots)
    def _():
        pltpu.make_async_copy(sib_hbm.at[term - slots], target, sem).start()


def left_kernel(phase, *refs):
    (own, sib, where, here, others, left, left_sib), refs = refs[:7], refs[7:]
    mixed, found, source, lbuf, obuf, lsem, osem = refs[-7:]
    slots, depth, outs = left.shape[0], lbuf.shape[0], obuf.shape[0]
    half = here.shape[1]
    bands = others.shape[0] + 1
    sector, band, core = where[phase], where[where.shape[0] - 2], where[where.shape[0] - 1]
    count = list_slots(own, sib, 0, sector, slots, found)

    def fetch(i, k):
        start_fetch(found[i], slots, left, left_sib, lbuf.at[k], lsem.at[k])

    def wait(k):
        pltpu.make_async_copy(left.at[0], lbuf.at[k], lsem.at[k]).wait()

    def out_copy(i, o):
        return pltpu.make_async_copy(obuf.at[o], mixed.at[found[i]], osem.at[o])

    def work(items, spots):
        for i, k in zip(items, spots):
            o = lax.rem(i, outs)

            @pl.when(i >= outs)
            def _():
                out_copy(i - outs, o).wait()

            obuf[o] = jnp.dot(lbuf[k], source[...], preferred_element_type=F32).astype(BF16)
            out_copy(i, o).start()

    for j in range(bands):
        b = lax.rem(band + j, bands)
        for i in range(CORES):
            c = core if i == 0 else 1 - core
            row = pl.multiple_of((b * CORES + c) * half, half)
            source[pl.ds(row, half)] = here[i] if j == 0 else others[j - 1, i]
    in_pairs(count, depth, fetch, wait, work)
    for back in range(outs, 0, -1):
        @pl.when(count >= back)
        def _():
            out_copy(count - back, lax.rem(count - back, outs)).wait()


def right_kernel(phase, *refs):
    own, sib, where, mixed, right, right_sib, keep, send, found, acc, mbuf, rbuf, msem, rsem = refs
    slots, depth = right.shape[0], rbuf.shape[0]
    half = keep.shape[1]
    bands = send.shape[0] + 1
    sector, band, core = where[phase], where[where.shape[0] - 2], where[where.shape[0] - 1]
    count = list_slots(own, sib, 1, sector, slots, found)

    def fetch(i, k):
        pltpu.make_async_copy(mixed.at[found[i]], mbuf.at[k], msem.at[k]).start()
        start_fetch(found[i], slots, right, right_sib, rbuf.at[k], rsem.at[k])

    def wait(k):
        pltpu.make_async_copy(mixed.at[0], mbuf.at[k], msem.at[k]).wait()
        pltpu.make_async_copy(right.at[0], rbuf.at[k], rsem.at[k]).wait()

    def work(items, spots):
        acc[...] += sum(
            lax.dot_general(mbuf[k], rbuf[k], (((1,), (1,)), ((), ())), preferred_element_type=F32) for k in spots
        )

    acc[...] = jnp.zeros_like(acc)
    in_pairs(count, depth, fetch, wait, work)
    for j in range(bands):
        b = lax.rem(band + j, bands)
        for i in range(CORES):
            c = core if i == 0 else 1 - core
            rows = acc[pl.ds(pl.multiple_of((b * CORES + c) * half, half), half)]
            if j == 0:
                keep[i] = rows
            else:
                send[j - 1, i] = rows.astype(BF16)


def local(devices, wavefunction, left, right, src, dst, live):
    slots, width = left.shape[0], left.shape[1]
    half = wavefunction.shape[0]
    sectors = half * devices // width
    bands = devices // (sectors * CORES)
    assert sectors == 4
    me = lax.axis_index("term")
    core, band, plane = me % CORES, (me // CORES) % bands, me // (CORES * bands)

    def move(value, to_plane=lambda a: a, band_step=0, flip=False):
        pairs = []
        for i in range(devices):
            c, b, a = i % CORES, (i // CORES) % bands, i // (CORES * bands)
            c = 1 - c if flip else c
            pairs.append((i, (to_plane(a) * bands + (b + band_step) % bands) * CORES + c))
        return lax.ppermute(value, "term", pairs)

    def beside(a):
        return a ^ 1

    def mirror(a):
        return 3 - a

    def bands_of(block):
        return jnp.stack([move(block, band_step=-j) for j in range(1, bands)])

    own_meta = jnp.concatenate([src, dst, live])
    sib_meta = move(own_meta, flip=True)
    mine = lax.dynamic_slice_in_dim(wavefunction, core * width, width, 1)
    theirs = lax.dynamic_slice_in_dim(wavefunction, (1 - core) * width, width, 1)
    from_sib = move(theirs, flip=True)
    left_sib, from_sib = lax.optimization_barrier((left, from_sib))
    left_sib = move(left_sib, flip=True)
    own_block = jnp.stack([mine, from_sib])
    mirror_block = move(own_block, mirror)
    own_bands, beside_block = bands_of(own_block), move(own_block, beside)
    beside_bands = bands_of(beside_block)
    blocks = [(own_block, own_bands), None, None, None]
    partner = plane ^ 1
    where_src = jnp.stack([plane, partner, 3 - plane, 3 - partner, band, core]).astype(jnp.int32)
    where_dst = jnp.stack([3 - partner, 3 - plane, partner, plane, band, core]).astype(jnp.int32)

    params = pltpu.CompilerParams(vmem_limit_bytes=VMEM)
    last_cost = pl.CostEstimate(flops=60 * 10**9, bytes_accessed=7 * width * width * 2, transcendentals=0)
    cost = pl.CostEstimate(flops=3 * 10**9, bytes_accessed=7 * width * width * 2, transcendentals=0)
    depth = 8
    mixed = None
    for phase in range(sectors):
        if phase == 1:
            mirror_block, mixed = lax.optimization_barrier((mirror_block, mixed))
            far_block = move(mirror_block, beside)
            mirror_block, beside_bands, right_sib = lax.optimization_barrier((mirror_block, beside_bands, right))
            right_sib = move(right_sib, flip=True)
            far_block, mirror_bands = lax.optimization_barrier((far_block, bands_of(mirror_block)))
            far_bands = bands_of(far_block)
            blocks[1:] = [(beside_block, beside_bands), (mirror_block, mirror_bands), (far_block, far_bands)]
        operands = [own_meta, sib_meta, where_src, *blocks[phase], left, left_sib]
        if mixed is not None:
            operands.append(mixed)
        mixed = pl.pallas_call(
            functools.partial(left_kernel, phase),
            out_shape=jax.ShapeDtypeStruct((CORES * slots, width, width), BF16),
            in_specs=[SMEM] * 3 + [WHOLE] * 2 + [ANY] * (len(operands) - 5),
            out_specs=ANY,
            scratch_shapes=[
                pltpu.SMEM((CORES * slots + 1,), jnp.int32),
                pltpu.VMEM((width, width), BF16),
                pltpu.VMEM((depth, width, width), BF16),
                pltpu.VMEM((4, width, width), BF16),
                pltpu.SemaphoreType.DMA((depth,)),
                pltpu.SemaphoreType.DMA((4,)),
            ],
            input_output_aliases={} if mixed is None else {7: 0},
            compiler_params=params,
            cost_estimate=last_cost if phase == sectors - 1 else cost,
            name="left_mix",
        )(*operands)

    def right_mix(phase, meta):
        keep, send = pl.pallas_call(
            functools.partial(right_kernel, phase),
            out_shape=(
                jax.ShapeDtypeStruct((CORES, half, width), F32),
                jax.ShapeDtypeStruct((bands - 1, CORES, half, width), BF16),
            ),
            in_specs=[SMEM] * 3 + [ANY] * 3,
            out_specs=(WHOLE, WHOLE),
            scratch_shapes=[
                pltpu.SMEM((CORES * slots + 1,), jnp.int32),
                pltpu.VMEM((width, width), F32),
                pltpu.VMEM((depth, width, width), BF16),
                pltpu.VMEM((depth, width, width), BF16),
                pltpu.SemaphoreType.DMA((depth,)),
                pltpu.SemaphoreType.DMA((depth,)),
            ],
            compiler_params=params,
            cost_estimate=cost,
            name="right_mix",
        )(meta, sib_meta, where_dst, mixed, right, right_sib)
        for j in range(1, bands):
            keep = keep + move(send[j - 1], band_step=j).astype(F32)
        return keep

    beside_far = right_mix(0, own_meta).astype(BF16)
    mirrored = right_mix(1, own_meta)
    mirrored = (mirrored + move(beside_far, beside).astype(F32)).astype(BF16)
    beside_near = right_mix(2, own_meta).astype(BF16)
    total = right_mix(3, own_meta) + move(mirrored, mirror).astype(F32) + move(beside_near, beside).astype(F32)
    same, cross = total[0], move(total[1], flip=True)
    first = core == 0
    return jnp.concatenate([jnp.where(first, same, cross), jnp.where(first, cross, same)], axis=1)


def solution(mesh):
    spec = P(("parts", "term"))
    return jax.shard_map(
        functools.partial(local, mesh.shape["term"]),
        mesh=mesh,
        in_specs=(spec,) * 6,
        out_specs=spec,
        check_vma=False,
    )
```

```python
import functools

import jax
import jax.numpy as jnp
from jax import lax
from jax.experimental import pallas as pl
from jax.experimental.pallas import tpu as pltpu
from jax.sharding import PartitionSpec as P

F32, BF16 = jnp.float32, jnp.bfloat16
CORES = 2
VMEM = 16 * 1024 * 1024
ANY = pl.BlockSpec(memory_space=pl.ANY)
SMEM = pl.BlockSpec(memory_space=pltpu.SMEM)
WHOLE = pl.BlockSpec(memory_space=pltpu.VMEM)


def list_slots(own, sib, field, sector, slots, found):
    count = jnp.int32(0)
    for core, meta in enumerate((own, sib)):
        live = meta[2 * slots]
        for t in range(slots):
            found[count] = core * slots + t
            hit = jnp.logical_and(t < live, meta[field * slots + t] == sector)
            count = count + hit.astype(jnp.int32)
    return count


def in_pairs(count, depth, fetch, wait, work):
    for i in range(depth - 2):
        @pl.when(i < count)
        def _():
            fetch(i, i)

    def pair(p, carry):
        i = 2 * p
        for ahead in (i + depth - 2, i + depth - 1):
            @pl.when(ahead < count)
            def _():
                fetch(ahead, lax.rem(ahead, depth))
        spots = [lax.rem(i, depth), lax.rem(i, depth) + 1]
        for k in spots:
            wait(k)
        work((i, i + 1), spots)
        return carry

    lax.fori_loop(0, count // 2, pair, 0)

    @pl.when(count % 2 == 1)
    def _():
        k = lax.rem(count - 1, depth)
        wait(k)
        work((count - 1,), (k,))


def start_fetch(term, slots, own_hbm, sib_hbm, target, sem):
    @pl.when(term < slots)
    def _():
        pltpu.make_async_copy(own_hbm.at[term], target, sem).start()

    @pl.when(term >= slots)
    def _():
        pltpu.make_async_copy(sib_hbm.at[term - slots], target, sem).start()


def left_kernel(phase, *refs):
    (own, sib, where, here, others, left, left_sib), refs = refs[:7], refs[7:]
    mixed, found, source, lbuf, obuf, lsem, osem = refs[-7:]
    slots, depth, outs = left.shape[0], lbuf.shape[0], obuf.shape[0]
    half = here.shape[1]
    bands = others.shape[0] + 1
    sector, band, core = where[phase], where[where.shape[0] - 2], where[where.shape[0] - 1]
    count = list_slots(own, sib, 0, sector, slots, found)

    def fetch(i, k):
        start_fetch(found[i], slots, left, left_sib, lbuf.at[k], lsem.at[k])

    def wait(k):
        pltpu.make_async_copy(left.at[0], lbuf.at[k], lsem.at[k]).wait()

    def out_copy(i, o):
        return pltpu.make_async_copy(obuf.at[o], mixed.at[found[i]], osem.at[o])

    def work(items, spots):
        for i, k in zip(items, spots):
            o = lax.rem(i, outs)

            @pl.when(i >= outs)
            def _():
                out_copy(i - outs, o).wait()

            obuf[o] = jnp.dot(lbuf[k], source[...], preferred_element_type=F32).astype(BF16)
            out_copy(i, o).start()

    for j in range(bands):
        b = lax.rem(band + j, bands)
        for i in range(CORES):
            c = core if i == 0 else 1 - core
            row = pl.multiple_of((b * CORES + c) * half, half)
            source[pl.ds(row, half)] = here[i] if j == 0 else others[j - 1, i]
    in_pairs(count, depth, fetch, wait, work)
    for back in range(outs, 0, -1):
        @pl.when(count >= back)
        def _():
            out_copy(count - back, lax.rem(count - back, outs)).wait()


def right_kernel(phase, *refs):
    own, sib, where, mixed, right, right_sib, keep, send, found, acc, mbuf, rbuf, msem, rsem = refs
    slots, depth = right.shape[0], rbuf.shape[0]
    half = keep.shape[1]
    bands = send.shape[0] + 1
    sector, band, core = where[phase], where[where.shape[0] - 2], where[where.shape[0] - 1]
    count = list_slots(own, sib, 1, sector, slots, found)

    def fetch(i, k):
        pltpu.make_async_copy(mixed.at[found[i]], mbuf.at[k], msem.at[k]).start()
        start_fetch(found[i], slots, right, right_sib, rbuf.at[k], rsem.at[k])

    def wait(k):
        pltpu.make_async_copy(mixed.at[0], mbuf.at[k], msem.at[k]).wait()
        pltpu.make_async_copy(right.at[0], rbuf.at[k], rsem.at[k]).wait()

    def work(items, spots):
        acc[...] += sum(
            lax.dot_general(mbuf[k], rbuf[k], (((1,), (1,)), ((), ())), preferred_element_type=F32) for k in spots
        )

    acc[...] = jnp.zeros_like(acc)
    in_pairs(count, depth, fetch, wait, work)
    for j in range(bands):
        b = lax.rem(band + j, bands)
        for i in range(CORES):
            c = core if i == 0 else 1 - core
            rows = acc[pl.ds(pl.multiple_of((b * CORES + c) * half, half), half)]
            if j == 0:
                keep[i] = rows
            else:
                send[j - 1, i] = rows.astype(BF16)


def local(devices, wavefunction, left, right, src, dst, live):
    slots, width = left.shape[0], left.shape[1]
    half = wavefunction.shape[0]
    sectors = half * devices // width
    bands = devices // (sectors * CORES)
    assert sectors == 4
    me = lax.axis_index("term")
    core, band, plane = me % CORES, (me // CORES) % bands, me // (CORES * bands)

    def move(value, to_plane=lambda a: a, band_step=0, flip=False):
        pairs = []
        for i in range(devices):
            c, b, a = i % CORES, (i // CORES) % bands, i // (CORES * bands)
            c = 1 - c if flip else c
            pairs.append((i, (to_plane(a) * bands + (b + band_step) % bands) * CORES + c))
        return lax.ppermute(value, "term", pairs)

    def beside(a):
        return a ^ 1

    def mirror(a):
        return 3 - a

    def bands_of(block):
        return jnp.stack([move(block, band_step=-j) for j in range(1, bands)])

    own_meta = jnp.concatenate([src, dst, live])
    sib_meta = move(own_meta, flip=True)
    mine = lax.dynamic_slice_in_dim(wavefunction, core * width, width, 1)
    theirs = lax.dynamic_slice_in_dim(wavefunction, (1 - core) * width, width, 1)
    from_sib = move(theirs, flip=True)
    left_sib, from_sib = lax.optimization_barrier((left, from_sib))
    left_sib = move(left_sib, flip=True)
    own_block = jnp.stack([mine, from_sib])
    mirror_block = move(own_block, mirror)
    own_bands, beside_block = bands_of(own_block), move(own_block, beside)
    beside_bands = bands_of(beside_block)
    blocks = [(own_block, own_bands), None, None, None]
    partner = plane ^ 1
    where_src = jnp.stack([plane, partner, 3 - plane, 3 - partner, band, core]).astype(jnp.int32)
    where_dst = jnp.stack([3 - partner, 3 - plane, partner, plane, band, core]).astype(jnp.int32)

    params = pltpu.CompilerParams(vmem_limit_bytes=VMEM)
    last_cost = pl.CostEstimate(flops=60 * 10**9, bytes_accessed=7 * width * width * 2, transcendentals=0)
    cost = pl.CostEstimate(flops=3 * 10**9, bytes_accessed=7 * width * width * 2, transcendentals=0)
    depth = 8
    mixed = None
    for phase in range(sectors):
        if phase == 1:
            mirror_block, mixed = lax.optimization_barrier((mirror_block, mixed))
            far_block = move(mirror_block, beside)
            mirror_block, beside_bands, right_sib = lax.optimization_barrier((mirror_block, beside_bands, right))
            right_sib = move(right_sib, flip=True)
            mirror_bands = bands_of(mirror_block)
            far_bands = bands_of(far_block)
            blocks[1:] = [(beside_block, beside_bands), (mirror_block, mirror_bands), (far_block, far_bands)]
        operands = [own_meta, sib_meta, where_src, *blocks[phase], left, left_sib]
        if mixed is not None:
            operands.append(mixed)
        mixed = pl.pallas_call(
            functools.partial(left_kernel, phase),
            out_shape=jax.ShapeDtypeStruct((CORES * slots, width, width), BF16),
            in_specs=[SMEM] * 3 + [WHOLE] * 2 + [ANY] * (len(operands) - 5),
            out_specs=ANY,
            scratch_shapes=[
                pltpu.SMEM((CORES * slots + 1,), jnp.int32),
                pltpu.VMEM((width, width), BF16),
                pltpu.VMEM((depth, width, width), BF16),
                pltpu.VMEM((4, width, width), BF16),
                pltpu.SemaphoreType.DMA((depth,)),
                pltpu.SemaphoreType.DMA((4,)),
            ],
            input_output_aliases={} if mixed is None else {7: 0},
            compiler_params=params,
            cost_estimate=last_cost if phase == sectors - 1 else cost,
            name="left_mix",
        )(*operands)

    def right_mix(phase, meta):
        keep, send = pl.pallas_call(
            functools.partial(right_kernel, phase),
            out_shape=(
                jax.ShapeDtypeStruct((CORES, half, width), F32),
                jax.ShapeDtypeStruct((bands - 1, CORES, half, width), BF16),
            ),
            in_specs=[SMEM] * 3 + [ANY] * 3,
            out_specs=(WHOLE, WHOLE),
            scratch_shapes=[
                pltpu.SMEM((CORES * slots + 1,), jnp.int32),
                pltpu.VMEM((width, width), F32),
                pltpu.VMEM((depth, width, width), BF16),
                pltpu.VMEM((depth, width, width), BF16),
                pltpu.SemaphoreType.DMA((depth,)),
                pltpu.SemaphoreType.DMA((depth,)),
            ],
            compiler_params=params,
            cost_estimate=cost,
            name="right_mix",
        )(meta, sib_meta, where_dst, mixed, right, right_sib)
        for j in range(1, bands):
            keep = keep + move(send[j - 1], band_step=j).astype(F32)
        return keep

    beside_far = right_mix(0, own_meta).astype(BF16)
    mirrored = right_mix(1, own_meta)
    meta, beside_far = lax.optimization_barrier((own_meta, beside_far))
    mirrored = (mirrored + move(beside_far, beside).astype(F32)).astype(BF16)
    beside_near = right_mix(2, meta).astype(BF16)
    total = right_mix(3, meta) + move(mirrored, mirror).astype(F32) + move(beside_near, beside).astype(F32)
    same, cross = total[0], move(total[1], flip=True)
    first = core == 0
    return jnp.concatenate([jnp.where(first, same, cross), jnp.where(first, cross, same)], axis=1)


def solution(mesh):
    spec = P(("parts", "term"))
    return jax.shard_map(
        functools.partial(local, mesh.shape["term"]),
        mesh=mesh,
        in_specs=(spec,) * 6,
        out_specs=spec,
        check_vma=False,
    )
```
